128 devices in a mesh: wide: 16 (over z_hi, y, core), narrow: 8 (over z_lo, x).
Axes of the slice: x: 4, y: 4, z: 4 (z_hi: 2, z_lo: 2; z = z_hi * 2 + z_lo), core: 2. Of those that a mesh axis runs over, the one named last changes fastest.
Arguments:
- weights_in: float32 [16, 64, 64, 2, 8, 128], P('wide', 'narrow'), may hold values from -6 to 6
- medium_speed: float32 [8, 8], replicated, may hold values from 0.5 to 2
- target_order: int32 [64], replicated, may hold values from 0 to 63, each once
Outputs:
- weights_out: float32 [16, 64, 64, 2, 8, 128], P('wide', 'narrow')
The draws below stay inside these ranges and needn't reach their ends.
Inputs may be any that keep to these rules, and one draw needn't show every extreme that they name: `target_order`: a permutation of the 64 starting target boxes.
All inputs are finite; a program needn't handle non-finite values.
Results may differ from the reference program's by a relative error of at most 0.0003.
Values sent between devices are 32-bit elements; how exact they have to be, the bound alone decides.
No kernel may reach another device: no remote copies, remote signals or barrier semaphores. Data moves between devices by JAX's collectives and lax.ppermute only.
A program may use at most 128 MiB of HBM per device.

```python
import jax
import jax.numpy as jnp
from jax import lax

PTS = 8
RHS = 16
TX = 8
TY = 8
SYH = 4
SX = 64
SY = 16
SH = 64
TB = 64


def block_scale(own_key, shape, shards, smallest, high):
    def one(axis_at, shards_of):
        draws = jax.random.uniform(jax.random.fold_in(jax.random.fold_in(own_key, 6), axis_at), (shards_of,), jnp.float32, smallest / len(shards), high / len(shards))
        return jnp.repeat(jnp.exp(draws), shape[axis_at] // shards_of).reshape((-1,) + (1,) * (len(shape) - axis_at - 1))

    gain = one(*shards[0])
    for cut in shards[1:]:
        gain = gain * one(*cut)
    return gain


def centred(stream_key, extent, width, limit, shards=(), kind=jnp.bfloat16):
    values = width * jax.random.normal(stream_key, extent, jnp.float32)
    if shards:
        values = values * block_scale(stream_key, extent, shards, -0.22, 0.18)
    return jnp.clip(values, -limit, limit).astype(kind)


def setup_inputs(seed: int = 0) -> dict:
    arg_keys = jax.random.split(jax.random.key(seed), 4)
    weights_in = centred(arg_keys[0], (16, SH, TB, 2, PTS, PTS * RHS), 1.0, 6.0, ((0, 16), (1, 8)), jnp.float32)
    medium_speed = jnp.clip(jax.random.uniform(arg_keys[1], (TX, TY), jnp.float32, 0.5, 2.0), 0.5, 2.0)
    target_order = jax.random.permutation(arg_keys[2], TB).astype(jnp.int32)
    return dict(weights_in=weights_in, medium_speed=medium_speed, target_order=target_order)


level_bits = (3, 2, 1, 0)
merges_across = (1, 1, 2, 2)
merges_down = (0, 1, 1, 2)

def cheb_nodes():
    counter = jnp.arange(8, dtype=jnp.float32)
    return 0.5 - 0.5 * jnp.cos(jnp.pi * (2.0 * counter + 1.0) / 16.0)

def lagrange_matrix(child_bit):
    node_set = cheb_nodes()
    points = (child_bit.astype(jnp.float32) + node_set) / 2.0
    differ = points[None, :, None] - node_set[None, None, :]
    spacing = node_set[:, None] - node_set[None, :]
    diagonal = jnp.eye(8, dtype=bool)
    factors = jnp.where(diagonal[:, None, :], 1.0, differ / jnp.where(diagonal, 1.0, spacing)[:, None, :])
    return jnp.prod(factors, axis=2)

def take_bit(number, position):
    return number >> position & 1

def phase_angles(step_index, box_code, target_bit, source_super, target_box, speed_rows, layout, child_bit):
    across_boxes, down_boxes, tiles_across, tiles_down, supers_down = layout
    own_bit = level_bits[step_index]
    shift_across = merges_across[step_index]
    shift_down = merges_down[step_index]
    chosen = box_code & 15 - (1 << own_bit) | target_bit << own_bit
    whole_across = 4 * (source_super // supers_down) + 2 * take_bit(box_code, 1) + take_bit(box_code, 3)
    whole_down = 4 * (source_super % supers_down) + 2 * take_bit(box_code, 0) + take_bit(box_code, 2)
    side_across = 2 ** shift_across / across_boxes
    side_down = 2 ** shift_down / down_boxes
    corner_across = (whole_across >> shift_across).astype(jnp.float32) * side_across
    corner_down = (whole_down >> shift_down).astype(jnp.float32) * side_down
    tile_across = target_box // tiles_down * 2 ** shift_across + (2 * take_bit(chosen, 3) + take_bit(chosen, 1) >> 2 - shift_across)
    tile_down = target_box % tiles_down * 2 ** shift_down + (2 * take_bit(chosen, 2) + take_bit(chosen, 0) >> 2 - shift_down)
    center_across = (tile_across.astype(jnp.float32) + 0.5) / (tiles_across * 2 ** shift_across)
    center_down = (tile_down.astype(jnp.float32) + 0.5) / (tiles_down * 2 ** shift_down)
    node_set = cheb_nodes()
    along_first = node_set
    along_second = node_set
    if child_bit is not None:
        halved = (child_bit.astype(jnp.float32) + node_set) / 2.0
        if step_index % 2 == 0:
            along_first = halved
        else:
            along_second = halved
    key_across = corner_across[..., None, None] + side_across * along_first[:, None]
    key_down = corner_down[..., None, None] + side_down * along_second[None, :]
    base_across = (corner_across + 0.5 * side_across)[..., None, None]
    base_down = (corner_down + 0.5 * side_down)[..., None, None]
    key_square = key_across * key_across + key_down * key_down
    base_square = base_across * base_across + base_down * base_down
    radial = (key_square - base_square) / (jnp.sqrt(key_square) + jnp.sqrt(base_square))
    wave_scale = jnp.pi * across_boxes / 2.0
    return wave_scale * (center_across[..., None, None] * (key_across - base_across) + center_down[..., None, None] * (key_down - base_down) + speed_rows[..., None, None] * radial)

def pull_child(weights, angles, step_index, child_bit):
    shaped = weights.reshape(weights.shape[:-3] + (2, 8, 8, 16))
    real_part = shaped[..., 0, :, :, :]
    imag_part = shaped[..., 1, :, :, :]
    cosine = jnp.cos(angles)[..., None]
    sine_part = jnp.sin(angles)[..., None]
    turned_real = real_part * cosine + imag_part * sine_part
    turned_imag = imag_part * cosine - real_part * sine_part
    stacked = jnp.stack([turned_real, turned_imag], axis=-4)
    matrix = lagrange_matrix(child_bit)
    if step_index % 2 == 0:
        moved = jnp.einsum('ab,...bcd->...acd', matrix, stacked, precision=lax.Precision.HIGHEST)
    else:
        moved = jnp.einsum('ab,...cbd->...cad', matrix, stacked, precision=lax.Precision.HIGHEST)
    return moved.reshape(weights.shape)

def push_parent(summed, angles):
    shaped = summed.reshape(summed.shape[:-3] + (2, 8, 8, 16))
    real_part = shaped[..., 0, :, :, :]
    imag_part = shaped[..., 1, :, :, :]
    cosine = jnp.cos(angles)[..., None]
    sine_part = jnp.sin(angles)[..., None]
    out_real = real_part * cosine - imag_part * sine_part
    out_imag = real_part * sine_part + imag_part * cosine
    return jnp.stack([out_real, out_imag], axis=-4).reshape(summed.shape)

def merge_local(weights, step_index, code_base, source_super, target_box, speed_rows, layout):
    code_count = weights.shape[0]
    own_bit = level_bits[step_index]
    low_span = 1 << own_bit
    high_span = code_count // (2 * low_span)
    trailing = weights.shape[1:-3]
    split_view = weights.reshape((high_span, 2, low_span) + weights.shape[1:])
    ones_tail = (1,) * len(trailing)
    high_index = jnp.arange(high_span, dtype=jnp.int32).reshape((high_span, 1) + ones_tail)
    low_index = jnp.arange(low_span, dtype=jnp.int32).reshape((1, low_span) + ones_tail)
    results = []
    for target_bit in (0, 1):
        target_value = jnp.asarray(target_bit, dtype=jnp.int32)
        summed = None
        for child in (0, 1):
            child_value = jnp.asarray(child, dtype=jnp.int32)
            box_code = code_base + high_index * (2 * low_span) + child * low_span + low_index
            angles = phase_angles(step_index, box_code, target_value, source_super, target_box, speed_rows, layout, child_value)
            term = pull_child(split_view[:, child], angles, step_index, child_value)
            summed = term if summed is None else summed + term
        parent_code = code_base + high_index * (2 * low_span) + low_index
        parent_angles = phase_angles(step_index, parent_code, target_value, source_super, target_box, speed_rows, layout, None)
        results.append(push_parent(summed, parent_angles))
    return jnp.stack(results, axis=1).reshape(weights.shape)

def reference(weights_in, medium_speed, target_order):
    layout = (SX, SY, TX, TY, SYH)
    speed_flat = medium_speed.reshape(-1)
    target_box = jnp.arange(TB, dtype=jnp.int32)

    def one_super(super_index):
        super_block = lax.dynamic_index_in_dim(weights_in, super_index, axis=1, keepdims=False)
        source_super = super_index.reshape(1)
        for step_index in range(4):
            super_block = merge_local(super_block, step_index, 0, source_super, target_box, speed_flat, layout)
        return jnp.take(super_block, target_order, axis=1)
    stacked = lax.map(one_super, jnp.arange(SH, dtype=jnp.int32))
    return jnp.transpose(stacked, (1, 2, 0, 3, 4, 5))
```

```python
import numpy as np
import jax
import jax.numpy as jnp
from jax import lax
from jax.experimental import pallas as pl
from jax.experimental.pallas import tpu as pltpu
from jax.sharding import PartitionSpec as P

SIN = (6.28318282, -41.3414214, 81.5961839, -76.5801007, 41.2053954, -12.2712631)
COS = (0.999999989, -19.7392045, 64.939119, -85.450166, 60.1678349, -25.9683235, 6.52962293)

NODES = 0.5 - 0.5 * np.cos(np.pi * (2.0 * np.arange(8) + 1.0) / 16.0)
TURNS = 16.0


def lagrange(child):
    points = (child + NODES) / 2.0
    out = np.ones((8, 8))
    for q in range(8):
        for m in range(8):
            if m != q:
                out[q] *= (points - NODES[m]) / (NODES[q] - NODES[m])
    return out


def turn(amount):
    return np.exp(2j * np.pi * TURNS * amount)


def dimension_operator(boxes):
    out = np.zeros((2, 2, 8, 2, 2, 8), complex)
    for ta in range(2):
        for tb in range(2):
            da, db = (2 * ta - 1) / 32.0, (2 * tb - 1) / 64.0
            last = turn((da + db) * 4.0 * NODES / boxes)
            for ca in range(2):
                for cb in range(2):
                    first = lagrange(ca) * turn(-da * (2 * cb + ca + NODES) / boxes)
                    second = lagrange(cb) * turn(-db * (2 * cb + 2 * NODES) / boxes)
                    out[ta, tb, :, ca, cb, :] = last[:, None] * (second @ first)
    return out


def halves(matrix):
    matrix = matrix.astype(np.float32)
    high = matrix.astype(jnp.bfloat16)
    low = (matrix - high.astype(np.float32)).astype(jnp.bfloat16)
    return high, low


def across_matrix():
    op = dimension_operator(64)
    real = np.zeros((2, 2, 2, 8, 2, 2, 2, 8))
    real[0, ..., 0, :] = op.real
    real[0, ..., 1, :] = -op.imag
    real[1, ..., 0, :] = op.imag
    real[1, ..., 1, :] = op.real
    high, low = halves(real.reshape(64, 64))
    return np.concatenate([high, high, low], axis=1)


def down_matrix():
    op = dimension_operator(16)
    real = np.zeros((2, 2, 2, 8, 2, 2, 2, 8))
    move = np.transpose(op, (3, 4, 5, 0, 1, 2))
    real[:, :, 0, :, 0] = move.real
    real[:, :, 1, :, 0] = -move.imag
    real[:, :, 0, :, 1] = move.imag
    real[:, :, 1, :, 1] = move.real
    flat = np.kron(real.reshape(64, 64), np.eye(16))
    return halves(flat)


def nodes_table():
    rows = np.repeat(NODES[:, None], 128, axis=1)
    lanes = np.repeat(np.repeat(NODES, 16)[None, :], 8, axis=0)
    return np.stack([rows, lanes]).astype(np.float32)


def horner(coefficients, x):
    total = jnp.full_like(x, coefficients[-1])
    for c in coefficients[-2::-1]:
        total = total * x + c
    return total


def unit(turns):
    rest = turns - jnp.round(turns)
    square = rest * rest
    return horner(COS, square), rest * horner(SIN, square)


def tables(nodes, super_index, first, second, count):
    sa = (super_index // 4).astype(jnp.float32)
    sd = (super_index % 4).astype(jnp.float32)
    local_a = first + count * nodes[0] - 2.0
    local_d = second + count * nodes[1] - 2.0
    mid_a, mid_d = 4.0 * sa + 2.0, 4.0 * sd + 2.0
    off_a, off_d = local_a / 64.0, local_d / 16.0
    key_a, key_d = (mid_a + local_a) / 64.0, (mid_d + local_d) / 16.0
    base_a, base_d = mid_a / 64.0, mid_d / 16.0
    key = jnp.sqrt(key_a * key_a + key_d * key_d)
    base = jnp.sqrt(jnp.zeros_like(key) + (base_a * base_a + base_d * base_d))
    radial = (off_a * (key_a + base_a) + off_d * (key_d + base_d)) / (key + base)
    return TURNS * off_a, TURNS * off_d, TURNS * radial


def turns_of(table, box, speed):
    center_a = ((box // 8).astype(jnp.float32) + 0.5) / 8.0
    center_d = ((box % 8).astype(jnp.float32) + 0.5) / 8.0
    return center_a * table[0] + center_d * table[1] + speed * table[2]


def pull_kernel(order_ref, speed_ref, nodes_ref, x_ref, o_ref):
    code = lax.axis_index("wide")
    super_index = lax.axis_index("narrow") * 8 + pl.program_id(0)
    bits = [(code >> k & 1).astype(jnp.float32) for k in range(4)]
    table = tables(nodes_ref, super_index, 2.0 * bits[1] + bits[3], 2.0 * bits[0] + bits[2], 1.0)

    def slot(place, carry):
        j = place // 4 % 8 * 8 + place // 32 * 4 + place % 4
        box = order_ref[j]
        cosine, sine = unit(turns_of(table, box, speed_ref[box]))
        real, imag = x_ref[0, box, 0], x_ref[0, box, 1]
        o_ref[0, place, 0] = real * cosine + imag * sine
        o_ref[0, place, 1] = imag * cosine - real * sine
        return carry

    lax.fori_loop(0, 64, slot, 0, unroll=8)


def split(value):
    high = value.astype(jnp.bfloat16)
    return high, (value - high.astype(jnp.float32)).astype(jnp.bfloat16)


def merge_kernel(pairs, order_ref, speed_ref, nodes_ref, across_ref, high_ref, low_ref, x_ref, o_ref, rows_h, rows_l):
    place = lax.axis_index("wide")
    super_index = lax.axis_index("narrow") * 8 + place // 2
    half = place % 2
    table = tables(nodes_ref, super_index, 0.0, 0.0, 4.0)
    across = across_ref[...]
    for g2 in range(2):
        for g0 in range(2):
            columns = []
            for p in range(pairs):
                parts = [x_ref[8 * g3 + 4 * g2 + 2 * g1 + g0, p].reshape(16, 128) for g3 in range(2) for g1 in range(2)]
                columns.append(jnp.concatenate(parts, axis=0))
            high, low = split(jnp.concatenate(columns, axis=1))
            moved = jnp.dot(across, jnp.concatenate([high, low, high], axis=0), preferred_element_type=jnp.float32)
            high, low = split(moved)
            for u in range(2):
                lane = 128 * (4 * g2 + 2 * g0 + u)
                for p in range(pairs):
                    rows_h[32 * p : 32 * p + 32, lane : lane + 128] = high[32 * u : 32 * u + 32, 128 * p : 128 * p + 128]
                    rows_l[32 * p : 32 * p + 32, lane : lane + 128] = low[32 * u : 32 * u + 32, 128 * p : 128 * p + 128]
    lanes = []
    for t2 in range(2):
        for t0 in range(2):
            result = []
            for u in range(2):
                lane = 128 * (4 * u + 2 * t2 + t0)
                wh, wl = high_ref[:, lane : lane + 128], low_ref[:, lane : lane + 128]
                result.append((wh, wl))
            wh = jnp.concatenate([result[0][0], result[1][0]], axis=1)
            wl = jnp.concatenate([result[0][1], result[1][1]], axis=1)
            total = jnp.dot(rows_h[...], wh, preferred_element_type=jnp.float32)
            total += jnp.dot(rows_l[...], wh, preferred_element_type=jnp.float32)
            total += jnp.dot(rows_h[...], wl, preferred_element_type=jnp.float32)
            lanes.append(total)
    for p in range(pairs):
        slot = pl.program_id(0) * pairs + p
        box = order_ref[slot // 4 * 8 + half * 4 + slot % 4]
        cosine, sine = unit(turns_of(table, box, speed_ref[box]))
        for t2 in range(2):
            for t0 in range(2):
                for t3 in range(2):
                    for t1 in range(2):
                        at = 32 * p + 16 * t3 + 8 * t1
                        block = lanes[2 * t2 + t0][at : at + 8]
                        real, imag = block[:, :128], block[:, 128:]
                        t = 8 * t3 + 4 * t2 + 2 * t1 + t0
                        o_ref[t, p, 0] = real * cosine - imag * sine
                        o_ref[t, p, 1] = real * sine + imag * cosine


SMEM = pl.BlockSpec(memory_space=pltpu.SMEM)


def whole(shape):
    return pl.BlockSpec(shape, lambda i: (0,) * len(shape))


def pull(order, speed, x):
    block = pl.BlockSpec((1, 64, 2, 8, 128), lambda i: (i, 0, 0, 0, 0))
    return pl.pallas_call(
        pull_kernel,
        grid=(8,),
        out_shape=jax.ShapeDtypeStruct((8, 64, 2, 8, 128), jnp.float32),
        in_specs=[SMEM, SMEM, whole((2, 8, 128)), block],
        out_specs=block,
        compiler_params=pltpu.CompilerParams(vmem_limit_bytes=32 * 2**20),
    )(order, speed, nodes_table(), x)


def merge(order, speed, x, pairs=16):
    high, low = down_matrix()
    block = pl.BlockSpec((16, pairs, 2, 8, 128), lambda i: (0, i, 0, 0, 0))
    return pl.pallas_call(
        lambda *refs: merge_kernel(pairs, *refs),
        grid=(32 // pairs,),
        out_shape=jax.ShapeDtypeStruct((16, 32, 2, 8, 128), jnp.float32),
        in_specs=[SMEM, SMEM, whole((2, 8, 128)), whole((64, 192)), whole((1024, 1024)), whole((1024, 1024)), block],
        out_specs=block,
        scratch_shapes=[pltpu.VMEM((32 * pairs, 1024), jnp.bfloat16)] * 2,
        compiler_params=pltpu.CompilerParams(vmem_limit_bytes=48 * 2**20),
    )(order, speed, nodes_table(), across_matrix(), high, low, x)


def local(weights_in, medium_speed, target_order):
    speed = medium_speed.reshape(-1)
    turned = pull(target_order, speed, weights_in[0])
    gathered = lax.all_to_all(turned.reshape(16, 32, 2, 8, 128), "wide", 0, 0)
    merged = merge(target_order, speed, gathered)
    spread = lax.all_to_all(merged.reshape(128, 4, 2, 8, 128), ("wide", "narrow"), 0, 0, tiled=True)
    spread = spread.reshape(8, 2, 8, 4, 2, 8, 128)
    return jnp.transpose(spread, (1, 3, 2, 0, 4, 5, 6)).reshape(1, 8, 64, 2, 8, 128)


def solution(mesh):
    in_specs = (P("wide", "narrow", None, None, None, None), P(), P())
    out_specs = P("wide", "narrow", None, None, None, None)
    return jax.shard_map(local, mesh=mesh, in_specs=in_specs, out_specs=out_specs, check_vma=False)
```

```python
import numpy as np
import jax
import jax.numpy as jnp
from jax import lax
from jax.experimental import pallas as pl
from jax.experimental.pallas import tpu as pltpu
from jax.sharding import PartitionSpec as P

SIN = (6.28318282, -41.3414214, 81.5961839, -76.5801007, 41.2053954, -12.2712631)
COS = (0.999999989, -19.7392045, 64.939119, -85.450166, 60.1678349, -25.9683235, 6.52962293)

NODES = 0.5 - 0.5 * np.cos(np.pi * (2.0 * np.arange(8) + 1.0) / 16.0)
TURNS = 16.0
SUPERS = 4


def lagrange(child):
    points = (child + NODES) / 2.0
    out = np.ones((8, 8))
    for q in range(8):
        for m in range(8):
            if m != q:
                out[q] *= (points - NODES[m]) / (NODES[q] - NODES[m])
    return out


def turn(amount):
    return np.exp(2j * np.pi * TURNS * amount)


def dimension_operator(boxes):
    out = np.zeros((2, 2, 8, 2, 2, 8), complex)
    for ta in range(2):
        for tb in range(2):
            da, db = (2 * ta - 1) / 32.0, (2 * tb - 1) / 64.0
            last = turn((da + db) * 4.0 * NODES / boxes)
            for ca in range(2):
                for cb in range(2):
                    first = lagrange(ca) * turn(-da * (2 * cb + ca + NODES) / boxes)
                    second = lagrange(cb) * turn(-db * (2 * cb + 2 * NODES) / boxes)
                    out[ta, tb, :, ca, cb, :] = last[:, None] * (second @ first)
    return out


def halves(matrix):
    matrix = matrix.astype(np.float32)
    high = matrix.astype(jnp.bfloat16)
    low = (matrix - high.astype(np.float32)).astype(jnp.bfloat16)
    return high, low


def across_matrix():
    op = dimension_operator(64)
    real = np.zeros((2, 2, 2, 8, 2, 2, 2, 8))
    real[0, ..., 0, :] = op.real
    real[0, ..., 1, :] = -op.imag
    real[1, ..., 0, :] = op.imag
    real[1, ..., 1, :] = op.real
    high, low = halves(real.reshape(64, 64))
    return np.concatenate([high, high, low], axis=1)


def down_matrix():
    op = dimension_operator(16)
    real = np.zeros((2, 2, 2, 8, 2, 2, 2, 8))
    move = np.transpose(op, (3, 4, 5, 0, 1, 2))
    real[:, :, 0, :, 0] = move.real
    real[:, :, 1, :, 0] = -move.imag
    real[:, :, 0, :, 1] = move.imag
    real[:, :, 1, :, 1] = move.real
    flat = np.kron(real.reshape(64, 64), np.eye(16))
    return halves(flat)


def spread_matrix():
    one = np.zeros((16, 8, 16, 8, 16))
    for box in range(16):
        one[box, np.arange(8), box, np.arange(8)] = 1.0
    one = one.reshape(128, 2048)
    return np.concatenate([one, one]).astype(jnp.bfloat16)


def horner(coefficients, x):
    total = jnp.full_like(x, coefficients[-1])
    for c in coefficients[-2::-1]:
        total = total * x + c
    return total


def unit(turns):
    rest = turns - jnp.round(turns)
    square = rest * rest
    return horner(COS, square), rest * horner(SIN, square)


def node_at(index):
    value = jnp.full(index.shape, NODES[0], jnp.float32)
    for q in range(1, 8):
        value = jnp.where(index == q, jnp.float32(NODES[q]), value)
    return value


def iota(axis):
    return lax.broadcasted_iota(jnp.int32, (8, 128), axis)


def tables(node_a, node_d, super_index, first, second, count):
    sa = (super_index // 4).astype(jnp.float32)
    sd = (super_index % 4).astype(jnp.float32)
    local_a = first + count * node_a - 2.0
    local_d = second + count * node_d - 2.0
    mid_a, mid_d = 4.0 * sa + 2.0, 4.0 * sd + 2.0
    off_a, off_d = local_a / 64.0, local_d / 16.0
    key_a, key_d = (mid_a + local_a) / 64.0, (mid_d + local_d) / 16.0
    base_a, base_d = mid_a / 64.0, mid_d / 16.0
    key = jnp.sqrt(key_a * key_a + key_d * key_d)
    base = jnp.sqrt(jnp.zeros_like(key) + (base_a * base_a + base_d * base_d))
    radial = (off_a * (key_a + base_a) + off_d * (key_d + base_d)) / (key + base)
    return TURNS * off_a, TURNS * off_d, TURNS * radial


def fetch(order_hbm, speed_hbm, order_ref, speed_ref, sems):
    copies = [
        pltpu.make_async_copy(order_hbm, order_ref, sems.at[0]),
        pltpu.make_async_copy(speed_hbm, speed_ref, sems.at[1]),
    ]
    for copy in copies:
        copy.start()
    for copy in copies:
        copy.wait()


def pull_kernel(order_hbm, speed_hbm, spread_ref, x_ref, o_ref, order_ref, speed_ref, place_ref, turned, sems):
    @pl.when(pl.program_id(0) == 0)
    def _():
        fetch(order_hbm, speed_hbm, order_ref, speed_ref, sems)
        for j in range(64):
            place_ref[order_ref[j]] = j % 8 // 4 * 32 + j // 8 * 4 + j % 4
        code = lax.axis_index("wide")
        bits = [(code >> k & 1).astype(jnp.float32) for k in range(4)]
        lane = iota(1)
        node_a, node_d = node_at(iota(0)), node_at(lane % 8)
        center_d = (lane // 8 % 8).astype(jnp.float32) / 8.0 + 0.0625
        center_a, speed = [], []
        for high in range(4):
            center_a.append((lane // 64 + 2 * high).astype(jnp.float32) / 8.0 + 0.0625)
            value = jnp.zeros((8, 128), jnp.float32)
            for low in range(16):
                value = jnp.where(lane // 8 == low, speed_ref[2 * high + low // 8, low % 8], value)
            speed.append(value)
        for s in range(8):
            super_index = lax.axis_index("narrow") * 8 + s
            table = tables(node_a, node_d, super_index, 2.0 * bits[1] + bits[3], 2.0 * bits[0] + bits[2], 1.0)
            turns = [center_a[h] * table[0] + (center_d * table[1] + speed[h] * table[2]) for h in range(4)]
            cosine, sine = unit(jnp.concatenate(turns, axis=0))
            high, low = split(jnp.concatenate([cosine, sine], axis=0))
            turned[s] = jnp.dot(
                jnp.concatenate([high, low], axis=1), spread_ref[...], preferred_element_type=jnp.float32
            )

    for s in range(SUPERS):
        at_super = pl.program_id(0) * SUPERS + s
        for box in range(64):
            place = place_ref[box]
            at, lane = 8 * (box // 16), 128 * (box % 16)
            cosine = turned[at_super, at : at + 8, lane : lane + 128]
            sine = turned[at_super, 32 + at : 40 + at, lane : lane + 128]
            real, imag = x_ref[s, box, 0], x_ref[s, box, 1]
            o_ref[s, place, 0] = real * cosine + imag * sine
            o_ref[s, place, 1] = imag * cosine - real * sine


def split(value):
    high = value.astype(jnp.bfloat16)
    return high, (value - high.astype(jnp.float32)).astype(jnp.bfloat16)


def merge_kernel(
    pairs, order_hbm, speed_hbm, across_ref, high_ref, low_ref, x_ref, o_ref, order_ref, speed_ref, rows_h, rows_l, sems
):
    @pl.when(pl.program_id(0) == 0)
    def _():
        fetch(order_hbm, speed_hbm, order_ref, speed_ref, sems)

    place = lax.axis_index("wide")
    super_index = lax.axis_index("narrow") * 8 + place // 2
    half = place % 2
    table = tables(node_at(iota(0)), node_at(iota(1) // 16), super_index, 0.0, 0.0, 4.0)
    across = across_ref[...]
    for g2 in range(2):
        for g0 in range(2):
            columns = []
            for p in range(pairs):
                parts = [x_ref[8 * g3 + 4 * g2 + 2 * g1 + g0, p].reshape(16, 128) for g3 in range(2) for g1 in range(2)]
                columns.append(jnp.concatenate(parts, axis=0))
            high, low = split(jnp.concatenate(columns, axis=1))
            moved = jnp.dot(across, jnp.concatenate([high, low, high], axis=0), preferred_element_type=jnp.float32)
            high, low = split(moved)
            for u in range(2):
                lane = 128 * (4 * g2 + 2 * g0 + u)
                for p in range(pairs):
                    rows_h[32 * p : 32 * p + 32, lane : lane + 128] = high[32 * u : 32 * u + 32, 128 * p : 128 * p + 128]
                    rows_l[32 * p : 32 * p + 32, lane : lane + 128] = low[32 * u : 32 * u + 32, 128 * p : 128 * p + 128]
    lanes = []
    for t2 in range(2):
        for t0 in range(2):
            result = []
            for u in range(2):
                lane = 128 * (4 * u + 2 * t2 + t0)
                wh, wl = high_ref[:, lane : lane + 128], low_ref[:, lane : lane + 128]
                result.append((wh, wl))
            wh = jnp.concatenate([result[0][0], result[1][0]], axis=1)
            wl = jnp.concatenate([result[0][1], result[1][1]], axis=1)
            total = jnp.dot(rows_h[...], wh, preferred_element_type=jnp.float32)
            total += jnp.dot(rows_l[...], wh, preferred_element_type=jnp.float32)
            total += jnp.dot(rows_h[...], wl, preferred_element_type=jnp.float32)
            lanes.append(total)
    for p in range(pairs):
        slot = pl.program_id(0) * pairs + p
        box = order_ref[slot // 4 * 8 + half * 4 + slot % 4]
        center_a = (box // 8).astype(jnp.float32) / 8.0 + 0.0625
        center_d = (box % 8).astype(jnp.float32) / 8.0 + 0.0625
        turns = center_a * table[0] + (center_d * table[1] + speed_ref[box // 8, box % 8] * table[2])
        cosine, sine = unit(turns)
        for t2 in range(2):
            for t0 in range(2):
                for t3 in range(2):
                    for t1 in range(2):
                        at = 32 * p + 16 * t3 + 8 * t1
                        block = lanes[2 * t2 + t0][at : at + 8]
                        real, imag = block[:, :128], block[:, 128:]
                        t = 8 * t3 + 4 * t2 + 2 * t1 + t0
                        o_ref[t, p, 0] = real * cosine - imag * sine
                        o_ref[t, p, 1] = real * sine + imag * cosine


ANY = pl.BlockSpec(memory_space=pl.ANY)
LOOKUP = [pltpu.SMEM((64,), jnp.int32), pltpu.SMEM((8, 8), jnp.float32)]


def whole(shape):
    return pl.BlockSpec(shape, lambda i: (0,) * len(shape))


def pull(order, speed, x):
    block = pl.BlockSpec((SUPERS, 64, 2, 8, 128), lambda i: (i, 0, 0, 0, 0))
    return pl.pallas_call(
        pull_kernel,
        grid=(8 // SUPERS,),
        out_shape=jax.ShapeDtypeStruct((8, 64, 2, 8, 128), jnp.float32),
        in_specs=[ANY, ANY, whole((256, 2048)), block],
        out_specs=block,
        scratch_shapes=LOOKUP
        + [pltpu.SMEM((64,), jnp.int32), pltpu.VMEM((8, 64, 2048), jnp.float32), pltpu.SemaphoreType.DMA((2,))],
        compiler_params=pltpu.CompilerParams(vmem_limit_bytes=60 * 2**20),
    )(order, speed, spread_matrix(), x)


def merge(order, speed, x, pairs=16):
    high, low = down_matrix()
    block = pl.BlockSpec((16, pairs, 2, 8, 128), lambda i: (0, i, 0, 0, 0))
    return pl.pallas_call(
        lambda *refs: merge_kernel(pairs, *refs),
        grid=(32 // pairs,),
        out_shape=jax.ShapeDtypeStruct((16, 32, 2, 8, 128), jnp.float32),
        in_specs=[ANY, ANY, whole((64, 192)), whole((1024, 1024)), whole((1024, 1024)), block],
        out_specs=block,
        scratch_shapes=LOOKUP + [pltpu.VMEM((32 * pairs, 1024), jnp.bfloat16)] * 2 + [pltpu.SemaphoreType.DMA((2,))],
        compiler_params=pltpu.CompilerParams(vmem_limit_bytes=48 * 2**20),
    )(order, speed, across_matrix(), high, low, x)


def local(weights_in, medium_speed, target_order):
    turned = pull(target_order, medium_speed, weights_in[0])
    gathered = lax.all_to_all(turned.reshape(16, 32, 2, 8, 128), "wide", 0, 0)
    merged = merge(target_order, medium_speed, gathered)
    spread = lax.all_to_all(merged.reshape(128, 4, 2, 8, 128), ("wide", "narrow"), 0, 0, tiled=True)
    spread = spread.reshape(8, 2, 8, 4, 2, 8, 128)
    return jnp.transpose(spread, (1, 3, 2, 0, 4, 5, 6)).reshape(1, 8, 64, 2, 8, 128)


def solution(mesh):
    in_specs = (P("wide", "narrow", None, None, None, None), P(), P())
    out_specs = P("wide", "narrow", None, None, None, None)
    return jax.shard_map(local, mesh=mesh, in_specs=in_specs, out_specs=out_specs, check_vma=False)
```

```python
import numpy as np
import jax
import jax.numpy as jnp
from jax import lax
from jax.experimental import pallas as pl
from jax.experimental.pallas import tpu as pltpu
from jax.sharding import Mesh, PartitionSpec as P

SIN = (6.28318282, -41.3414214, 81.5961839, -76.5801007, 41.2053954, -12.2712631)
COS = (0.999999989, -19.7392045, 64.939119, -85.450166, 60.1678349, -25.9683235, 6.52962293)

NODES = 0.5 - 0.5 * np.cos(np.pi * (2.0 * np.arange(8) + 1.0) / 16.0)
TURNS = 16.0
FINE = ("z_hi", "y", "core", "z_lo", "x")
FINE_SIZES = (2, 4, 2, 2, 4)
WIDE, NARROW = FINE[:3], FINE[3:]


def lagrange(child):
    points = (child + NODES) / 2.0
    out = np.ones((8, 8))
    for q in range(8):
        for m in range(8):
            if m != q:
                out[q] *= (points - NODES[m]) / (NODES[q] - NODES[m])
    return out


def turn(amount):
    return np.exp(2j * np.pi * TURNS * amount)


def dimension_operator(boxes):
    out = np.zeros((2, 2, 8, 2, 2, 8), complex)
    for ta in range(2):
        for tb in range(2):
            da, db = (2 * ta - 1) / 32.0, (2 * tb - 1) / 64.0
            last = turn((da + db) * 4.0 * NODES / boxes)
            for ca in range(2):
                for cb in range(2):
                    first = lagrange(ca) * turn(-da * (2 * cb + ca + NODES) / boxes)
                    second = lagrange(cb) * turn(-db * (2 * cb + 2 * NODES) / boxes)
                    out[ta, tb, :, ca, cb, :] = last[:, None] * (second @ first)
    return out


def halves(matrix):
    matrix = matrix.astype(np.float32)
    high = matrix.astype(jnp.bfloat16)
    low = (matrix - high.astype(np.float32)).astype(jnp.bfloat16)
    return high, low


def across_matrix():
    op = dimension_operator(64)
    real = np.zeros((2, 2, 2, 8, 2, 2, 2, 8))
    real[0, ..., 0, :] = op.real
    real[0, ..., 1, :] = -op.imag
    real[1, ..., 0, :] = op.imag
    real[1, ..., 1, :] = op.real
    high, low = halves(real.reshape(64, 64))
    return np.concatenate([high, high, low], axis=1)


def down_matrix():
    move = np.transpose(dimension_operator(16), (3, 4, 5, 0, 1, 2))[:, :, :, 0]
    real = np.stack([move.real, move.imag], axis=4)
    return halves(np.kron(real.reshape(32, 32), np.eye(16)))


def spread_matrix():
    one = np.zeros((16, 8, 16, 8, 16))
    for box in range(16):
        one[box, np.arange(8), box, np.arange(8)] = 1.0
    one = one.reshape(128, 2048)
    return np.concatenate([one, one]).astype(jnp.bfloat16)


def horner(coefficients, x):
    total = jnp.full_like(x, coefficients[-1])
    for c in coefficients[-2::-1]:
        total = total * x + c
    return total


def unit(turns):
    rest = turns - jnp.round(turns)
    square = rest * rest
    return horner(COS, square), rest * horner(SIN, square)


def node_at(index):
    value = jnp.full(index.shape, NODES[0], jnp.float32)
    for q in range(1, 8):
        value = jnp.where(index == q, jnp.float32(NODES[q]), value)
    return value


def iota(axis):
    return lax.broadcasted_iota(jnp.int32, (8, 128), axis)


def tables(node_a, node_d, super_index, first, second, count):
    sa = (super_index // 4).astype(jnp.float32)
    sd = (super_index % 4).astype(jnp.float32)
    local_a = first + count * node_a - 2.0
    local_d = second + count * node_d - 2.0
    mid_a, mid_d = 4.0 * sa + 2.0, 4.0 * sd + 2.0
    off_a, off_d = local_a / 64.0, local_d / 16.0
    key_a, key_d = (mid_a + local_a) / 64.0, (mid_d + local_d) / 16.0
    base_a, base_d = mid_a / 64.0, mid_d / 16.0
    key = jnp.sqrt(key_a * key_a + key_d * key_d)
    base = jnp.sqrt(jnp.zeros_like(key) + (base_a * base_a + base_d * base_d))
    radial = (off_a * (key_a + base_a) + off_d * (key_d + base_d)) / (key + base)
    return TURNS * off_a, TURNS * off_d, TURNS * radial


def fetch(order_hbm, speed_hbm, order_ref, speed_ref, sems):
    copies = [
        pltpu.make_async_copy(order_hbm, order_ref, sems.at[0]),
        pltpu.make_async_copy(speed_hbm, speed_ref, sems.at[1]),
    ]
    for copy in copies:
        copy.start()
    for copy in copies:
        copy.wait()


def wide_code():
    return lax.axis_index("z_hi") * 8 + lax.axis_index("y") * 2 + lax.axis_index("core")


def narrow_place():
    return lax.axis_index("z_lo") * 4 + lax.axis_index("x")


def pull_kernel(
    order_hbm, speed_hbm, spread_ref, x_hbm, o_hbm, order_ref, speed_ref, place_ref, x_ref, o_ref, turned, sems, in_sems, out_sems
):
    arrivals = [pltpu.make_async_copy(x_hbm.at[s], x_ref.at[s], in_sems.at[s]) for s in range(8)]
    for arrival in arrivals:
        arrival.start()
    fetch(order_hbm, speed_hbm, order_ref, speed_ref, sems)
    for j in range(64):
        place_ref[order_ref[j]] = j % 8 * 8 + j // 8
    code = wide_code()
    bits = [(code >> k & 1).astype(jnp.float32) for k in range(4)]
    lane = iota(1)
    node_a, node_d = node_at(iota(0)), node_at(lane % 8)
    center_d = (lane // 8 % 8).astype(jnp.float32) / 8.0 + 0.0625
    center_a, speed = [], []
    for high in range(4):
        center_a.append((lane // 64 + 2 * high).astype(jnp.float32) / 8.0 + 0.0625)
        value = jnp.zeros((8, 128), jnp.float32)
        for low in range(16):
            value = jnp.where(lane // 8 == low, speed_ref[2 * high + low // 8, low % 8], value)
        speed.append(value)
    departures = []
    flat = o_ref.reshape(512, 2, 8, 128)
    for s in range(8):
        super_index = narrow_place() * 8 + s
        table = tables(node_a, node_d, super_index, 2.0 * bits[1] + bits[3], 2.0 * bits[0] + bits[2], 1.0)
        turns = [center_a[h] * table[0] + (center_d * table[1] + speed[h] * table[2]) for h in range(4)]
        cosine, sine = unit(jnp.concatenate(turns, axis=0))
        high, low = split(jnp.concatenate([cosine, sine], axis=0))
        turned[s] = jnp.dot(jnp.concatenate([high, low], axis=1), spread_ref[...], preferred_element_type=jnp.float32)
        arrivals[s].wait()
        for box in range(64):
            place = place_ref[box] + 64 * s
            at, lanes = 8 * (box // 16), 128 * (box % 16)
            cosine = turned[s, at : at + 8, lanes : lanes + 128]
            sine = turned[s, 32 + at : 40 + at, lanes : lanes + 128]
            real, imag = x_ref[s, box, 0], x_ref[s, box, 1]
            flat[place, 0] = real * cosine + imag * sine
            flat[place, 1] = imag * cosine - real * sine
        departure = pltpu.make_async_copy(o_ref.at[s], o_hbm.at[:, s], out_sems.at[s])
        departure.start()
        departures.append(departure)
    for departure in departures:
        departure.wait()


def split(value):
    high = value.astype(jnp.bfloat16)
    return high, (value - high.astype(jnp.float32)).astype(jnp.bfloat16)


def merge_kernel(
    tiles, order_hbm, speed_hbm, across_ref, high_ref, low_ref, x_ref, o_ref, order_ref, speed_ref, rows_h, rows_l, sems
):
    @pl.when(pl.program_id(0) == 0)
    def _():
        fetch(order_hbm, speed_hbm, order_ref, speed_ref, sems)

    code = wide_code()
    across = across_ref[...]
    pairs = [(tile, s) for tile in range(tiles) for s in range(4)]
    for g2 in range(2):
        for g0 in range(2):
            columns = []
            for tile, s in pairs:
                parts = [
                    x_ref[8 * g3 + 4 * g2 + 2 * g1 + g0, s, tile].reshape(16, 128) for g3 in range(2) for g1 in range(2)
                ]
                columns.append(jnp.concatenate(parts, axis=0))
            high, low = split(jnp.concatenate(columns, axis=1))
            moved = jnp.dot(across, jnp.concatenate([high, low, high], axis=0), preferred_element_type=jnp.float32)
            high, low = split(moved)
            lane = 128 * (2 * g2 + g0)
            for p in range(len(pairs)):
                rows_h[64 * p : 64 * p + 64, lane : lane + 128] = high[:, 128 * p : 128 * p + 128]
                rows_l[64 * p : 64 * p + 64, lane : lane + 128] = low[:, 128 * p : 128 * p + 128]
    table = [
        tables(node_at(iota(0)), node_at(iota(1) // 16), narrow_place() * 8 + code % 2 * 4 + s, 0.0, 0.0, 4.0)
        for s in range(4)
    ]
    units = []
    for tile, s in pairs:
        box = order_ref[(pl.program_id(0) * tiles + tile) * 8 + code // 2]
        center_a = (box // 8).astype(jnp.float32) / 8.0 + 0.0625
        center_d = (box % 8).astype(jnp.float32) / 8.0 + 0.0625
        speed = speed_ref[box // 8, box % 8]
        units.append(unit(center_a * table[s][0] + (center_d * table[s][1] + speed * table[s][2])))
    for t0 in range(2):
        wh, wl = high_ref[:, 256 * t0 : 256 * t0 + 256], low_ref[:, 256 * t0 : 256 * t0 + 256]
        total = jnp.dot(rows_h[...], wh, preferred_element_type=jnp.float32)
        total += jnp.dot(rows_l[...], wh, preferred_element_type=jnp.float32)
        total += jnp.dot(rows_h[...], wl, preferred_element_type=jnp.float32)
        for p, (tile, s) in enumerate(pairs):
            cosine, sine = units[p]
            for t3 in range(2):
                for t1 in range(2):
                    at = 64 * p + 16 * t3 + 8 * t1
                    by_re, by_im = total[at : at + 8], total[at + 32 : at + 40]
                    real_re, real_im = by_re[:, :128], by_re[:, 128:]
                    imag_re, imag_im = by_im[:, :128], by_im[:, 128:]
                    for t2, real, imag in (
                        (0, real_re - imag_im, imag_re + real_im),
                        (1, real_re + imag_im, imag_re - real_im),
                    ):
                        low = t0 if t2 == 0 else 1 - t0
                        o_ref[4 * t3 + 2 * t2 + t1, tile, low, s, 0] = real * cosine - imag * sine
                        o_ref[4 * t3 + 2 * t2 + t1, tile, low, s, 1] = real * sine + imag * cosine


ANY = pl.BlockSpec(memory_space=pl.ANY)
LOOKUP = [pltpu.SMEM((64,), jnp.int32), pltpu.SMEM((8, 8), jnp.float32)]


def whole(shape):
    return pl.BlockSpec(shape, lambda i: (0,) * len(shape))


def pull(order, speed, x):
    return pl.pallas_call(
        pull_kernel,
        out_shape=jax.ShapeDtypeStruct((8, 8, 8, 2, 8, 128), jnp.float32),
        in_specs=[ANY, ANY, pl.BlockSpec(memory_space=pltpu.VMEM), ANY],
        out_specs=ANY,
        scratch_shapes=LOOKUP
        + [
            pltpu.SMEM((64,), jnp.int32),
            pltpu.VMEM((8, 64, 2, 8, 128), jnp.float32),
            pltpu.VMEM((8, 8, 8, 2, 8, 128), jnp.float32),
            pltpu.VMEM((8, 64, 2048), jnp.float32),
            pltpu.SemaphoreType.DMA((2,)),
            pltpu.SemaphoreType.DMA((8,)),
            pltpu.SemaphoreType.DMA((8,)),
        ],
        compiler_params=pltpu.CompilerParams(vmem_limit_bytes=60 * 2**20),
    )(order, speed, spread_matrix(), x)


def merge(order, speed, x, tiles=2):
    high, low = down_matrix()
    return pl.pallas_call(
        lambda *refs: merge_kernel(tiles, *refs),
        grid=(8 // tiles,),
        out_shape=jax.ShapeDtypeStruct((8, 8, 2, 4, 2, 8, 128), jnp.float32),
        in_specs=[
            ANY,
            ANY,
            whole((64, 192)),
            whole((512, 512)),
            whole((512, 512)),
            pl.BlockSpec((16, 4, tiles, 2, 8, 128), lambda i: (0, 0, i, 0, 0, 0)),
        ],
        out_specs=pl.BlockSpec((8, tiles, 2, 4, 2, 8, 128), lambda i: (0, i, 0, 0, 0, 0, 0)),
        scratch_shapes=LOOKUP
        + [pltpu.VMEM((256 * tiles, 512), jnp.bfloat16)] * 2
        + [pltpu.SemaphoreType.DMA((2,))],
        compiler_params=pltpu.CompilerParams(vmem_limit_bytes=48 * 2**20),
    )(order, speed, across_matrix(), high, low, x)


def local(weights_in, medium_speed, target_order):
    turned = pull(target_order, medium_speed, weights_in[0])
    gathered = lax.all_to_all(turned.reshape(16, 4, 8, 2, 8, 128), WIDE, 0, 0, tiled=True)
    merged = merge(target_order, medium_speed, gathered)
    chunks = merged.reshape(128, 4, 2, 8, 128)
    spread = lax.all_to_all(chunks, ("z_hi", "y", "z_lo", "x", "core"), 0, 0, tiled=True)
    return spread.reshape(1, 8, 64, 2, 8, 128)


def solution(mesh):
    fine = Mesh(mesh.devices.reshape(FINE_SIZES), FINE)
    split_over = P(WIDE, NARROW, None, None, None, None)
    return jax.shard_map(local, mesh=fine, in_specs=(split_over, P(), P()), out_specs=split_over, check_vma=False)
```

```python
import numpy as np
import jax
import jax.numpy as jnp
from jax import lax
from jax.experimental import pallas as pl
from jax.experimental.pallas import tpu as pltpu
from jax.sharding import Mesh, PartitionSpec as P

SIN = (6.28318282, -41.3414214, 81.5961839, -76.5801007, 41.2053954, -12.2712631)
COS = (0.999999989, -19.7392045, 64.939119, -85.450166, 60.1678349, -25.9683235, 6.52962293)

NODES = 0.5 - 0.5 * np.cos(np.pi * (2.0 * np.arange(8) + 1.0) / 16.0)
TURNS = 16.0
FINE = ("z_hi", "y", "core", "z_lo", "x")
FINE_SIZES = (2, 4, 2, 2, 4)
WIDE, NARROW = FINE[:3], FINE[3:]


def lagrange(child):
    points = (child + NODES) / 2.0
    out = np.ones((8, 8))
    for q in range(8):
        for m in range(8):
            if m != q:
                out[q] *= (points - NODES[m]) / (NODES[q] - NODES[m])
    return out


def turn(amount):
    return np.exp(2j * np.pi * TURNS * amount)


def dimension_operator(boxes):
    out = np.zeros((2, 2, 8, 2, 2, 8), complex)
    for ta in range(2):
        for tb in range(2):
            da, db = (2 * ta - 1) / 32.0, (2 * tb - 1) / 64.0
            last = turn((da + db) * 4.0 * NODES / boxes)
            for ca in range(2):
                for cb in range(2):
                    first = lagrange(ca) * turn(-da * (2 * cb + ca + NODES) / boxes)
                    second = lagrange(cb) * turn(-db * (2 * cb + 2 * NODES) / boxes)
                    out[ta, tb, :, ca, cb, :] = last[:, None] * (second @ first)
    return out


def halves(matrix):
    matrix = matrix.astype(np.float32)
    high = matrix.astype(jnp.bfloat16)
    low = (matrix - high.astype(np.float32)).astype(jnp.bfloat16)
    return high, low


def across_matrix():
    op = dimension_operator(64)
    real = np.zeros((2, 2, 2, 8, 2, 2, 2, 8))
    real[0, ..., 0, :] = op.real
    real[0, ..., 1, :] = -op.imag
    real[1, ..., 0, :] = op.imag
    real[1, ..., 1, :] = op.real
    high, low = halves(real.reshape(64, 64))
    return np.concatenate([high, high, low], axis=1)


def down_matrix():
    move = np.transpose(dimension_operator(16), (3, 4, 5, 0, 1, 2))[:, :, :, 0]
    real = np.stack([move.real, move.imag], axis=4)
    return halves(np.kron(real.reshape(32, 32), np.eye(16)))


def spread_matrix():
    one = np.zeros((16, 8, 16, 8, 16))
    for box in range(16):
        one[box, np.arange(8), box, np.arange(8)] = 1.0
    return one.reshape(128, 2048).astype(jnp.bfloat16)


def horner(coefficients, x):
    total = jnp.full_like(x, coefficients[-1])
    for c in coefficients[-2::-1]:
        total = total * x + c
    return total


def unit(turns):
    rest = turns - jnp.round(turns)
    square = rest * rest
    return horner(COS, square), rest * horner(SIN, square)


def node_at(index):
    value = jnp.full(index.shape, NODES[0], jnp.float32)
    for q in range(1, 8):
        value = jnp.where(index == q, jnp.float32(NODES[q]), value)
    return value


def iota(axis):
    return lax.broadcasted_iota(jnp.int32, (8, 128), axis)


def tables(node_a, node_d, super_index, first, second, count):
    sa = (super_index // 4).astype(jnp.float32)
    sd = (super_index % 4).astype(jnp.float32)
    local_a = first + count * node_a - 2.0
    local_d = second + count * node_d - 2.0
    mid_a, mid_d = 4.0 * sa + 2.0, 4.0 * sd + 2.0
    off_a, off_d = local_a / 64.0, local_d / 16.0
    key_a, key_d = (mid_a + local_a) / 64.0, (mid_d + local_d) / 16.0
    base_a, base_d = mid_a / 64.0, mid_d / 16.0
    key = jnp.sqrt(key_a * key_a + key_d * key_d)
    base = jnp.sqrt(jnp.zeros_like(key) + (base_a * base_a + base_d * base_d))
    radial = (off_a * (key_a + base_a) + off_d * (key_d + base_d)) / (key + base)
    return TURNS * off_a, TURNS * off_d, TURNS * radial


def fetch(sources, targets, sems):
    copies = [pltpu.make_async_copy(*pair, sems.at[k]) for k, pair in enumerate(zip(sources, targets))]
    for copy in copies:
        copy.start()
    return copies


def wide_code():
    return lax.axis_index("z_hi") * 8 + lax.axis_index("y") * 2 + lax.axis_index("core")


def narrow_place():
    return lax.axis_index("z_lo") * 4 + lax.axis_index("x")


def pull_kernel(
    order_hbm,
    speed_hbm,
    spread_hbm,
    x_hbm,
    o_hbm,
    order_ref,
    speed_ref,
    place_ref,
    spread_ref,
    x_ref,
    o_ref,
    turned,
    sems,
    in_sems,
    out_sems,
):
    lookups = fetch((order_hbm, speed_hbm, spread_hbm), (order_ref, speed_ref, spread_ref), sems)
    arrivals = [pltpu.make_async_copy(x_hbm.at[s], x_ref.at[s], in_sems.at[s]) for s in range(8)]
    for arrival in arrivals:
        arrival.start()
    code = wide_code()
    bits = [(code >> k & 1).astype(jnp.float32) for k in range(4)]
    lane = iota(1)
    node_a, node_d = node_at(iota(0)), node_at(lane % 8)
    center_a = [(lane // 64 + 2 * high).astype(jnp.float32) / 8.0 + 0.0625 for high in range(4)]
    center_d = (lane // 8 % 8).astype(jnp.float32) / 8.0 + 0.0625
    plane, radial = [], []
    for s in range(8):
        super_index = narrow_place() * 8 + s
        table = tables(node_a, node_d, super_index, 2.0 * bits[1] + bits[3], 2.0 * bits[0] + bits[2], 1.0)
        plane.append([center_a[high] * table[0] + center_d * table[1] for high in range(4)])
        radial.append(table[2])
    lookups[1].wait()
    speed = []
    for high in range(4):
        value = jnp.zeros((8, 128), jnp.float32)
        for low in range(16):
            value = jnp.where(lane // 8 == low, speed_ref[2 * high + low // 8, low % 8], value)
        speed.append(value)
    lookups[0].wait()
    for j in range(64):
        place_ref[order_ref[j]] = j % 8 * 8 + j // 8
    lookups[2].wait()

    def spread(group):
        both_supers = (2 * group, 2 * group + 1)
        angles = [plane[s][high] + speed[high] * radial[s] for s in both_supers for high in range(4)]
        cosine, sine = unit(jnp.concatenate(angles, axis=0))
        high, low = split(jnp.concatenate([cosine[:32], sine[:32], cosine[32:], sine[32:]], axis=0))
        both = jnp.dot(jnp.concatenate([high, low], axis=0), spread_ref[...], preferred_element_type=jnp.float32)
        turned[128 * group : 128 * group + 128] = both[:128] + both[128:]

    spread(0)
    departures = []
    flat = o_ref.reshape(512, 2, 8, 128)
    for s in range(8):
        arrivals[s].wait()
        if s % 2 == 1 and s < 7:
            spread(s // 2 + 1)
        for box in range(64):
            place = place_ref[box] + 64 * s
            at, lanes = 64 * s + 8 * (box // 16), 128 * (box % 16)
            cosine = turned[at : at + 8, lanes : lanes + 128]
            sine = turned[32 + at : 40 + at, lanes : lanes + 128]
            real, imag = x_ref[s, box, 0], x_ref[s, box, 1]
            flat[place, 0] = real * cosine + imag * sine
            flat[place, 1] = imag * cosine - real * sine
        departure = pltpu.make_async_copy(o_ref.at[s], o_hbm.at[:, s], out_sems.at[s])
        departure.start()
        departures.append(departure)
    for departure in departures:
        departure.wait()


def split(value):
    high = value.astype(jnp.bfloat16)
    return high, (value - high.astype(jnp.float32)).astype(jnp.bfloat16)


def merge_kernel(
    tiles, order_hbm, speed_hbm, across_ref, high_ref, low_ref, x_ref, o_ref, order_ref, speed_ref, rows, sems
):
    @pl.when(pl.program_id(0) == 0)
    def _():
        for copy in fetch((order_hbm, speed_hbm), (order_ref, speed_ref), sems):
            copy.wait()

    code = wide_code()
    across = across_ref[...]
    pairs = [(tile, s) for tile in range(tiles) for s in range(4)]
    size = 64 * len(pairs)
    for g2 in range(2):
        for g0 in range(2):
            columns = []
            for tile, s in pairs:
                parts = [
                    x_ref[8 * g3 + 4 * g2 + 2 * g1 + g0, s, tile].reshape(16, 128) for g3 in range(2) for g1 in range(2)
                ]
                columns.append(jnp.concatenate(parts, axis=0))
            high, low = split(jnp.concatenate(columns, axis=1))
            moved = jnp.dot(across, jnp.concatenate([high, low, high], axis=0), preferred_element_type=jnp.float32)
            high, low = split(moved)
            lane = 128 * (2 * g2 + g0)
            for p in range(len(pairs)):
                rows[64 * p : 64 * p + 64, lane : lane + 128] = high[:, 128 * p : 128 * p + 128]
                rows[size + 64 * p : size + 64 * p + 64, lane : lane + 128] = low[:, 128 * p : 128 * p + 128]
    table = [
        tables(node_at(iota(0)), node_at(iota(1) // 16), narrow_place() * 8 + code % 2 * 4 + s, 0.0, 0.0, 4.0)
        for s in range(4)
    ]
    units = []
    for tile, s in pairs:
        box = order_ref[(pl.program_id(0) * tiles + tile) * 8 + code // 2]
        center_a = (box // 8).astype(jnp.float32) / 8.0 + 0.0625
        center_d = (box % 8).astype(jnp.float32) / 8.0 + 0.0625
        speed = speed_ref[box // 8, box % 8]
        units.append(unit(center_a * table[s][0] + (center_d * table[s][1] + speed * table[s][2])))
    for t0 in range(2):
        wh, wl = high_ref[:, 256 * t0 : 256 * t0 + 256], low_ref[:, 256 * t0 : 256 * t0 + 256]
        both = jnp.dot(rows[...], wh, preferred_element_type=jnp.float32)
        total = both[:size] + both[size:] + jnp.dot(rows[:size], wl, preferred_element_type=jnp.float32)
        for p, (tile, s) in enumerate(pairs):
            cosine, sine = units[p]
            for t3 in range(2):
                for t1 in range(2):
                    at = 64 * p + 16 * t3 + 8 * t1
                    by_re, by_im = total[at : at + 8], total[at + 32 : at + 40]
                    real_re, real_im = by_re[:, :128], by_re[:, 128:]
                    imag_re, imag_im = by_im[:, :128], by_im[:, 128:]
                    for t2, real, imag in (
                        (0, real_re - imag_im, imag_re + real_im),
                        (1, real_re + imag_im, imag_re - real_im),
                    ):
                        low = t0 if t2 == 0 else 1 - t0
                        o_ref[4 * t3 + 2 * t2 + t1, tile, low, s, 0] = real * cosine - imag * sine
                        o_ref[4 * t3 + 2 * t2 + t1, tile, low, s, 1] = real * sine + imag * cosine


ANY = pl.BlockSpec(memory_space=pl.ANY)
LOOKUP = [pltpu.SMEM((64,), jnp.int32), pltpu.SMEM((8, 8), jnp.float32)]


def whole(shape):
    return pl.BlockSpec(shape, lambda i: (0,) * len(shape))


def pull(order, speed, x):
    return pl.pallas_call(
        pull_kernel,
        out_shape=jax.ShapeDtypeStruct((8, 8, 8, 2, 8, 128), jnp.float32),
        in_specs=[ANY, ANY, ANY, ANY],
        out_specs=ANY,
        scratch_shapes=LOOKUP
        + [
            pltpu.SMEM((64,), jnp.int32),
            pltpu.VMEM((128, 2048), jnp.bfloat16),
            pltpu.VMEM((8, 64, 2, 8, 128), jnp.float32),
            pltpu.VMEM((8, 8, 8, 2, 8, 128), jnp.float32),
            pltpu.VMEM((512, 2048), jnp.float32),
            pltpu.SemaphoreType.DMA((3,)),
            pltpu.SemaphoreType.DMA((8,)),
            pltpu.SemaphoreType.DMA((8,)),
        ],
        compiler_params=pltpu.CompilerParams(vmem_limit_bytes=60 * 2**20),
    )(order, speed, spread_matrix(), x)


def merge(order, speed, x, tiles=2):
    high, low = down_matrix()
    return pl.pallas_call(
        lambda *refs: merge_kernel(tiles, *refs),
        grid=(8 // tiles,),
        out_shape=jax.ShapeDtypeStruct((8, 8, 2, 4, 2, 8, 128), jnp.float32),
        in_specs=[
            ANY,
            ANY,
            whole((64, 192)),
            whole((512, 512)),
            whole((512, 512)),
            pl.BlockSpec((16, 4, tiles, 2, 8, 128), lambda i: (0, 0, i, 0, 0, 0)),
        ],
        out_specs=pl.BlockSpec((8, tiles, 2, 4, 2, 8, 128), lambda i: (0, i, 0, 0, 0, 0, 0)),
        scratch_shapes=LOOKUP
        + [pltpu.VMEM((512 * tiles, 512), jnp.bfloat16)]
        + [pltpu.SemaphoreType.DMA((2,))],
        compiler_params=pltpu.CompilerParams(vmem_limit_bytes=32 * 2**20),
    )(order, speed, across_matrix(), high, low, x)


def local(weights_in, medium_speed, target_order):
    turned = pull(target_order, medium_speed, weights_in[0])
    gathered = lax.all_to_all(turned.reshape(16, 4, 8, 2, 8, 128), WIDE, 0, 0, tiled=True)
    merged = merge(target_order, medium_speed, gathered)
    chunks = merged.reshape(128, 4, 2, 8, 128)
    spread = lax.all_to_all(chunks, ("z_hi", "y", "z_lo", "x", "core"), 0, 0, tiled=True)
    return spread.reshape(1, 8, 64, 2, 8, 128)


def solution(mesh):
    fine = Mesh(mesh.devices.reshape(FINE_SIZES), FINE)
    split_over = P(WIDE, NARROW, None, None, None, None)
    return jax.shard_map(local, mesh=fine, in_specs=(split_over, P(), P()), out_specs=split_over, check_vma=False)
```

```python
import numpy as np
import jax
import jax.numpy as jnp
from jax import lax
from jax.experimental import pallas as pl
from jax.experimental.pallas import tpu as pltpu
from jax.sharding import Mesh, PartitionSpec as P

SIN = (6.28318282, -41.3414214, 81.5961839, -76.5801007, 41.2053954, -12.2712631)
COS = (0.999999989, -19.7392045, 64.939119, -85.450166, 60.1678349, -25.9683235, 6.52962293)

NODES = 0.5 - 0.5 * np.cos(np.pi * (2.0 * np.arange(8) + 1.0) / 16.0)
TURNS = 16.0
FINE = ("z_hi", "y", "core", "z_lo", "x")
FINE_SIZES = (2, 4, 2, 2, 4)
WIDE, NARROW = FINE[:3], FINE[3:]


def lagrange(child):
    points = (child + NODES) / 2.0
    out = np.ones((8, 8))
    for q in range(8):
        for m in range(8):
            if m != q:
                out[q] *= (points - NODES[m]) / (NODES[q] - NODES[m])
    return out


def turn(amount):
    return np.exp(2j * np.pi * TURNS * amount)


def dimension_operator(boxes):
    out = np.zeros((2, 2, 8, 2, 2, 8), complex)
    for ta in range(2):
        for tb in range(2):
            da, db = (2 * ta - 1) / 32.0, (2 * tb - 1) / 64.0
            last = turn((da + db) * 4.0 * NODES / boxes)
            for ca in range(2):
                for cb in range(2):
                    first = lagrange(ca) * turn(-da * (2 * cb + ca + NODES) / boxes)
                    second = lagrange(cb) * turn(-db * (2 * cb + 2 * NODES) / boxes)
                    out[ta, tb, :, ca, cb, :] = last[:, None] * (second @ first)
    return out


def halves(matrix):
    matrix = matrix.astype(np.float32)
    high = matrix.astype(jnp.bfloat16)
    low = (matrix - high.astype(np.float32)).astype(jnp.bfloat16)
    return high, low


def across_matrix():
    op = dimension_operator(64)
    real = np.zeros((2, 2, 2, 8, 2, 2, 2, 8))
    real[0, ..., 0, :] = op.real
    real[0, ..., 1, :] = -op.imag
    real[1, ..., 0, :] = op.imag
    real[1, ..., 1, :] = op.real
    high, low = halves(real.reshape(64, 64))
    return np.concatenate([high, high, low], axis=1)


def down_matrix():
    move = np.transpose(dimension_operator(16), (3, 4, 5, 0, 1, 2))[:, :, :, 0]
    real = np.stack([move.real, move.imag], axis=4)
    return halves(np.kron(real.reshape(32, 32), np.eye(16)))


def horner(coefficients, x):
    total = jnp.full_like(x, coefficients[-1])
    for c in coefficients[-2::-1]:
        total = total * x + c
    return total


def unit(turns):
    rest = turns - jnp.round(turns)
    square = rest * rest
    return horner(COS, square), rest * horner(SIN, square)


def node_at(index):
    value = jnp.full(index.shape, NODES[0], jnp.float32)
    for q in range(1, 8):
        value = jnp.where(index == q, jnp.float32(NODES[q]), value)
    return value


def iota(axis):
    return lax.broadcasted_iota(jnp.int32, (8, 128), axis)


def tables(node_a, node_d, super_index, first, second, count):
    sa = (super_index // 4).astype(jnp.float32)
    sd = (super_index % 4).astype(jnp.float32)
    local_a = first + count * node_a - 2.0
    local_d = second + count * node_d - 2.0
    mid_a, mid_d = 4.0 * sa + 2.0, 4.0 * sd + 2.0
    off_a, off_d = local_a / 64.0, local_d / 16.0
    key_a, key_d = (mid_a + local_a) / 64.0, (mid_d + local_d) / 16.0
    base_a, base_d = mid_a / 64.0, mid_d / 16.0
    key = jnp.sqrt(key_a * key_a + key_d * key_d)
    base = jnp.sqrt(jnp.zeros_like(key) + (base_a * base_a + base_d * base_d))
    radial = (off_a * (key_a + base_a) + off_d * (key_d + base_d)) / (key + base)
    return TURNS * off_a, TURNS * off_d, TURNS * radial


def wide_code():
    return lax.axis_index("z_hi") * 8 + lax.axis_index("y") * 2 + lax.axis_index("core")


def narrow_place():
    return lax.axis_index("z_lo") * 4 + lax.axis_index("x")


def pull_kernel(
    lookup_hbm, x_hbm, o_hbm, lookup_ref, place_ref, spread_ref, x_ref, o_ref, turned, sem, in_sems, out_sems
):
    lookup = pltpu.make_async_copy(lookup_hbm, lookup_ref, sem)
    lookup.start()
    arrivals = [pltpu.make_async_copy(x_hbm.at[s], x_ref.at[s], in_sems.at[s]) for s in range(8)]
    for arrival in arrivals:
        arrival.start()
    code = wide_code()
    bits = [(code >> k & 1).astype(jnp.float32) for k in range(4)]
    lane = iota(1)
    node_a, node_d = node_at(iota(0)), node_at(lane % 8)
    center_a = [(lane // 64 + 2 * high).astype(jnp.float32) / 8.0 + 0.0625 for high in range(4)]
    center_d = (lane // 8 % 8).astype(jnp.float32) / 8.0 + 0.0625
    plane, radial = [], []
    for s in range(8):
        super_index = narrow_place() * 8 + s
        table = tables(node_a, node_d, super_index, 2.0 * bits[1] + bits[3], 2.0 * bits[0] + bits[2], 1.0)
        plane.append([center_a[high] * table[0] + center_d * table[1] for high in range(4)])
        radial.append(table[2])
    spread_ref[...] = jnp.zeros_like(spread_ref)
    row = lax.broadcasted_iota(jnp.int32, (16, 128), 0)
    point = lax.broadcasted_iota(jnp.int32, (16, 128), 1) // 16
    for box in range(16):
        same = jnp.where(row == box % 2 * 8 + point, 1.0, 0.0).astype(jnp.bfloat16)
        spread_ref[box // 2 * 16 : box // 2 * 16 + 16, 128 * box : 128 * box + 128] = same
    lookup.wait()
    speed = []
    for high in range(4):
        value = jnp.zeros((8, 128), jnp.float32)
        for low in range(16):
            value = jnp.where(lane // 8 == low, lookup_ref[2 * high + low // 8, low % 8], value)
        speed.append(value)
    for j in range(64):
        place_ref[lookup_ref[8, j].astype(jnp.int32)] = j % 8 * 8 + j // 8

    def spread(group):
        both_supers = (2 * group, 2 * group + 1)
        angles = [plane[s][high] + speed[high] * radial[s] for s in both_supers for high in range(4)]
        cosine, sine = unit(jnp.concatenate(angles, axis=0))
        high, low = split(jnp.concatenate([cosine[:32], sine[:32], cosine[32:], sine[32:]], axis=0))
        both = jnp.dot(jnp.concatenate([high, low], axis=0), spread_ref[...], preferred_element_type=jnp.float32)
        turned[128 * group : 128 * group + 128] = both[:128] + both[128:]

    spread(0)
    departures = []
    flat = o_ref.reshape(512, 2, 8, 128)
    for s in range(8):
        arrivals[s].wait()
        if s % 2 == 1 and s < 7:
            spread(s // 2 + 1)
        for box in range(64):
            place = place_ref[box] + 64 * s
            at, lanes = 64 * s + 8 * (box // 16), 128 * (box % 16)
            cosine = turned[at : at + 8, lanes : lanes + 128]
            sine = turned[32 + at : 40 + at, lanes : lanes + 128]
            real, imag = x_ref[s, box, 0], x_ref[s, box, 1]
            flat[place, 0] = real * cosine + imag * sine
            flat[place, 1] = imag * cosine - real * sine
        departure = pltpu.make_async_copy(o_ref.at[s], o_hbm.at[:, s], out_sems.at[s])
        departure.start()
        departures.append(departure)
    for departure in departures:
        departure.wait()


def split(value):
    high = value.astype(jnp.bfloat16)
    return high, (value - high.astype(jnp.float32)).astype(jnp.bfloat16)


def merge_kernel(
    tiles, lookup_hbm, across_ref, high_ref, low_ref, x_ref, o_ref, lookup_ref, rows, sem
):
    @pl.when(pl.program_id(0) == 0)
    def _():
        lookup = pltpu.make_async_copy(lookup_hbm, lookup_ref, sem)
        lookup.start()
        lookup.wait()

    code = wide_code()
    across = across_ref[...]
    pairs = [(tile, s) for tile in range(tiles) for s in range(4)]
    size = 64 * len(pairs)
    for g2 in range(2):
        for g0 in range(2):
            columns = []
            for tile, s in pairs:
                parts = [
                    x_ref[8 * g3 + 4 * g2 + 2 * g1 + g0, s, tile].reshape(16, 128) for g3 in range(2) for g1 in range(2)
                ]
                columns.append(jnp.concatenate(parts, axis=0))
            high, low = split(jnp.concatenate(columns, axis=1))
            moved = jnp.dot(across, jnp.concatenate([high, low, high], axis=0), preferred_element_type=jnp.float32)
            high, low = split(moved)
            lane = 128 * (2 * g2 + g0)
            for p in range(len(pairs)):
                rows[64 * p : 64 * p + 64, lane : lane + 128] = high[:, 128 * p : 128 * p + 128]
                rows[size + 64 * p : size + 64 * p + 64, lane : lane + 128] = low[:, 128 * p : 128 * p + 128]
    table = [
        tables(node_at(iota(0)), node_at(iota(1) // 16), narrow_place() * 8 + code % 2 * 4 + s, 0.0, 0.0, 4.0)
        for s in range(4)
    ]
    units = []
    for tile, s in pairs:
        box = lookup_ref[8, (pl.program_id(0) * tiles + tile) * 8 + code // 2].astype(jnp.int32)
        center_a = (box // 8).astype(jnp.float32) / 8.0 + 0.0625
        center_d = (box % 8).astype(jnp.float32) / 8.0 + 0.0625
        speed = lookup_ref[box // 8, box % 8]
        units.append(unit(center_a * table[s][0] + (center_d * table[s][1] + speed * table[s][2])))
    for t0 in range(2):
        wh, wl = high_ref[:, 256 * t0 : 256 * t0 + 256], low_ref[:, 256 * t0 : 256 * t0 + 256]
        both = jnp.dot(rows[...], wh, preferred_element_type=jnp.float32)
        total = both[:size] + both[size:] + jnp.dot(rows[:size], wl, preferred_element_type=jnp.float32)
        for p, (tile, s) in enumerate(pairs):
            cosine, sine = units[p]
            for t3 in range(2):
                for t1 in range(2):
                    at = 64 * p + 16 * t3 + 8 * t1
                    by_re, by_im = total[at : at + 8], total[at + 32 : at + 40]
                    real_re, real_im = by_re[:, :128], by_re[:, 128:]
                    imag_re, imag_im = by_im[:, :128], by_im[:, 128:]
                    for t2, real, imag in (
                        (0, real_re - imag_im, imag_re + real_im),
                        (1, real_re + imag_im, imag_re - real_im),
                    ):
                        low = t0 if t2 == 0 else 1 - t0
                        o_ref[4 * t3 + 2 * t2 + t1, tile, low, s, 0] = real * cosine - imag * sine
                        o_ref[4 * t3 + 2 * t2 + t1, tile, low, s, 1] = real * sine + imag * cosine


ANY = pl.BlockSpec(memory_space=pl.ANY)
LOOKUP = pltpu.SMEM((9, 64), jnp.float32)


def whole(shape):
    return pl.BlockSpec(shape, lambda i: (0,) * len(shape))


def pull(lookup, x):
    return pl.pallas_call(
        pull_kernel,
        out_shape=jax.ShapeDtypeStruct((8, 8, 8, 2, 8, 128), jnp.float32),
        in_specs=[ANY, ANY],
        out_specs=ANY,
        scratch_shapes=[
            LOOKUP,
            pltpu.SMEM((64,), jnp.int32),
            pltpu.VMEM((128, 2048), jnp.bfloat16),
            pltpu.VMEM((8, 64, 2, 8, 128), jnp.float32),
            pltpu.VMEM((8, 8, 8, 2, 8, 128), jnp.float32),
            pltpu.VMEM((512, 2048), jnp.float32),
            pltpu.SemaphoreType.DMA,
            pltpu.SemaphoreType.DMA((8,)),
            pltpu.SemaphoreType.DMA((8,)),
        ],
        compiler_params=pltpu.CompilerParams(vmem_limit_bytes=48 * 2**20),
    )(lookup, x)


def merge(lookup, x, tiles=2):
    high, low = down_matrix()
    return pl.pallas_call(
        lambda *refs: merge_kernel(tiles, *refs),
        grid=(8 // tiles,),
        out_shape=jax.ShapeDtypeStruct((8, 8, 2, 4, 2, 8, 128), jnp.float32),
        in_specs=[
            ANY,
            whole((64, 192)),
            whole((512, 512)),
            whole((512, 512)),
            pl.BlockSpec((16, 4, tiles, 2, 8, 128), lambda i: (0, 0, i, 0, 0, 0)),
        ],
        out_specs=pl.BlockSpec((8, tiles, 2, 4, 2, 8, 128), lambda i: (0, i, 0, 0, 0, 0, 0)),
        scratch_shapes=[LOOKUP, pltpu.VMEM((512 * tiles, 512), jnp.bfloat16), pltpu.SemaphoreType.DMA],
        compiler_params=pltpu.CompilerParams(vmem_limit_bytes=32 * 2**20),
    )(lookup, across_matrix(), high, low, x)


def local(weights_in, medium_speed, target_order):
    speeds = jnp.pad(medium_speed, ((0, 0), (0, 56)))
    lookup = jnp.concatenate([speeds, target_order.astype(jnp.float32)[None]], axis=0)
    turned = pull(lookup, weights_in[0])
    gathered = lax.all_to_all(turned.reshape(16, 4, 8, 2, 8, 128), WIDE, 0, 0, tiled=True)
    merged = merge(lookup, gathered)
    chunks = merged.reshape(128, 4, 2, 8, 128)
    spread = lax.all_to_all(chunks, ("z_hi", "y", "z_lo", "x", "core"), 0, 0, tiled=True)
    return spread.reshape(1, 8, 64, 2, 8, 128)


def solution(mesh):
    fine = Mesh(mesh.devices.reshape(FINE_SIZES), FINE)
    split_over = P(WIDE, NARROW, None, None, None, None)
    return jax.shard_map(local, mesh=fine, in_specs=(split_over, P(), P()), out_specs=split_over, check_vma=False)
```

```python
import numpy as np
import jax
import jax.numpy as jnp
from jax import lax
from jax.experimental import pallas as pl
from jax.experimental.pallas import tpu as pltpu
from jax.sharding import Mesh, PartitionSpec as P

SIN = (6.28318282, -41.3414214, 81.5961839, -76.5801007, 41.2053954, -12.2712631)
COS = (0.999999989, -19.7392045, 64.939119, -85.450166, 60.1678349, -25.9683235, 6.52962293)

NODES = 0.5 - 0.5 * np.cos(np.pi * (2.0 * np.arange(8) + 1.0) / 16.0)
TURNS = 16.0
FINE = ("z_hi", "y", "core", "z_lo", "x")
FINE_SIZES = (2, 4, 2, 2, 4)
WIDE, NARROW = FINE[:3], FINE[3:]


def lagrange(child):
    points = (child + NODES) / 2.0
    out = np.ones((8, 8))
    for q in range(8):
        for m in range(8):
            if m != q:
                out[q] *= (points - NODES[m]) / (NODES[q] - NODES[m])
    return out


def turn(amount):
    return np.exp(2j * np.pi * TURNS * amount)


def dimension_operator(boxes):
    out = np.zeros((2, 2, 8, 2, 2, 8), complex)
    for ta in range(2):
        for tb in range(2):
            da, db = (2 * ta - 1) / 32.0, (2 * tb - 1) / 64.0
            last = turn((da + db) * 4.0 * NODES / boxes)
            for ca in range(2):
                for cb in range(2):
                    first = lagrange(ca) * turn(-da * (2 * cb + ca + NODES) / boxes)
                    second = lagrange(cb) * turn(-db * (2 * cb + 2 * NODES) / boxes)
                    out[ta, tb, :, ca, cb, :] = last[:, None] * (second @ first)
    return out


def halves(matrix):
    matrix = matrix.astype(np.float32)
    high = matrix.astype(jnp.bfloat16)
    low = (matrix - high.astype(np.float32)).astype(jnp.bfloat16)
    return high, low


def across_matrix():
    op = dimension_operator(64)
    real = np.zeros((2, 2, 2, 8, 2, 2, 2, 8))
    real[0, ..., 0, :] = op.real
    real[0, ..., 1, :] = -op.imag
    real[1, ..., 0, :] = op.imag
    real[1, ..., 1, :] = op.real
    high, low = halves(real.reshape(64, 64))
    return np.concatenate([high, high, low], axis=1)


def down_matrix():
    move = np.transpose(dimension_operator(16), (3, 4, 5, 0, 1, 2))[:, :, :, 0]
    real = np.stack([move.real, move.imag], axis=4)
    return halves(np.kron(real.reshape(32, 32), np.eye(16)))


def horner(coefficients, x):
    total = jnp.full_like(x, coefficients[-1])
    for c in coefficients[-2::-1]:
        total = total * x + c
    return total


def unit(turns):
    rest = turns - jnp.round(turns)
    square = rest * rest
    return horner(COS, square), rest * horner(SIN, square)


def node_at(index):
    value = jnp.full(index.shape, NODES[0], jnp.float32)
    for q in range(1, 8):
        value = jnp.where(index == q, jnp.float32(NODES[q]), value)
    return value


def iota(axis):
    return lax.broadcasted_iota(jnp.int32, (8, 128), axis)


def tables(node_a, node_d, super_index, first, second, count):
    sa = (super_index // 4).astype(jnp.float32)
    sd = (super_index % 4).astype(jnp.float32)
    local_a = first + count * node_a - 2.0
    local_d = second + count * node_d - 2.0
    mid_a, mid_d = 4.0 * sa + 2.0, 4.0 * sd + 2.0
    off_a, off_d = local_a / 64.0, local_d / 16.0
    key_a, key_d = (mid_a + local_a) / 64.0, (mid_d + local_d) / 16.0
    base_a, base_d = mid_a / 64.0, mid_d / 16.0
    key = jnp.sqrt(key_a * key_a + key_d * key_d)
    base = jnp.sqrt(jnp.zeros_like(key) + (base_a * base_a + base_d * base_d))
    radial = (off_a * (key_a + base_a) + off_d * (key_d + base_d)) / (key + base)
    return TURNS * off_a, TURNS * off_d, TURNS * radial


def wide_code():
    return lax.axis_index("z_hi") * 8 + lax.axis_index("y") * 2 + lax.axis_index("core")


def narrow_place():
    return lax.axis_index("z_lo") * 4 + lax.axis_index("x")


def pull_kernel(
    lookup_hbm,
    x_hbm,
    o_hbm,
    push_hbm,
    lookup_ref,
    place_ref,
    spread_ref,
    x_ref,
    o_ref,
    push_ref,
    turned,
    sem,
    push_sem,
    in_sems,
    out_sems,
):
    lookup = pltpu.make_async_copy(lookup_hbm, lookup_ref, sem)
    lookup.start()
    arrivals = [pltpu.make_async_copy(x_hbm.at[s], x_ref.at[s], in_sems.at[s]) for s in range(8)]
    for arrival in arrivals:
        arrival.start()
    code = wide_code()
    bits = [(code >> k & 1).astype(jnp.float32) for k in range(4)]
    lane = iota(1)
    node_a, node_d = node_at(iota(0)), node_at(lane % 8)
    center_a = [(lane // 64 + 2 * high).astype(jnp.float32) / 8.0 + 0.0625 for high in range(4)]
    center_d = (lane // 8 % 8).astype(jnp.float32) / 8.0 + 0.0625
    plane, radial = [], []
    for s in range(8):
        super_index = narrow_place() * 8 + s
        table = tables(node_a, node_d, super_index, 2.0 * bits[1] + bits[3], 2.0 * bits[0] + bits[2], 1.0)
        plane.append([center_a[high] * table[0] + center_d * table[1] for high in range(4)])
        radial.append(table[2])
    spread_ref[...] = jnp.zeros_like(spread_ref)
    row = lax.broadcasted_iota(jnp.int32, (16, 128), 0)
    point = lax.broadcasted_iota(jnp.int32, (16, 128), 1) // 16
    for box in range(16):
        same = jnp.where(row == box % 2 * 8 + point, 1.0, 0.0).astype(jnp.bfloat16)
        spread_ref[box // 2 * 16 : box // 2 * 16 + 16, 128 * box : 128 * box + 128] = same
    lookup.wait()
    speed = []
    for high in range(4):
        value = jnp.zeros((8, 128), jnp.float32)
        for low in range(16):
            value = jnp.where(lane // 8 == low, lookup_ref[2 * high + low // 8, low % 8], value)
        speed.append(value)
    for j in range(64):
        place_ref[lookup_ref[8, j].astype(jnp.int32)] = j % 8 * 8 + j // 8

    def spread(group):
        both_supers = (2 * group, 2 * group + 1)
        angles = [plane[s][high] + speed[high] * radial[s] for s in both_supers for high in range(4)]
        cosine, sine = unit(jnp.concatenate(angles, axis=0))
        high, low = split(jnp.concatenate([cosine[:32], sine[:32], cosine[32:], sine[32:]], axis=0))
        both = jnp.dot(jnp.concatenate([high, low], axis=0), spread_ref[...], preferred_element_type=jnp.float32)
        turned[128 * group : 128 * group + 128] = both[:128] + both[128:]

    spread(0)
    table = [
        tables(node_a, node_at(lane // 16), narrow_place() * 8 + code % 2 * 4 + s, 0.0, 0.0, 4.0) for s in range(4)
    ]
    for tile in range(8):
        box = lookup_ref[8, tile * 8 + code // 2].astype(jnp.int32)
        across = (box // 8).astype(jnp.float32) / 8.0 + 0.0625
        down = (box % 8).astype(jnp.float32) / 8.0 + 0.0625
        at_box = lookup_ref[box // 8, box % 8]
        for s in range(4):
            cosine, sine = unit(across * table[s][0] + (down * table[s][1] + at_box * table[s][2]))
            push_ref[tile, s, 0] = cosine
            push_ref[tile, s, 1] = sine
    push_copy = pltpu.make_async_copy(push_ref, push_hbm, push_sem)
    push_copy.start()
    departures = []
    flat = o_ref.reshape(512, 2, 8, 128)
    for s in range(8):
        arrivals[s].wait()
        if s % 2 == 1 and s < 7:
            spread(s // 2 + 1)
        for box in range(64):
            place = place_ref[box] + 64 * s
            at, lanes = 64 * s + 8 * (box // 16), 128 * (box % 16)
            cosine = turned[at : at + 8, lanes : lanes + 128]
            sine = turned[32 + at : 40 + at, lanes : lanes + 128]
            real, imag = x_ref[s, box, 0], x_ref[s, box, 1]
            flat[place, 0] = real * cosine + imag * sine
            flat[place, 1] = imag * cosine - real * sine
        departure = pltpu.make_async_copy(o_ref.at[s], o_hbm.at[:, s], out_sems.at[s])
        departure.start()
        departures.append(departure)
    push_copy.wait()
    for departure in departures:
        departure.wait()


def split(value):
    high = value.astype(jnp.bfloat16)
    return high, (value - high.astype(jnp.float32)).astype(jnp.bfloat16)


def merge_kernel(
    tiles, push_ref, across_ref, high_ref, low_ref, x_ref, o_ref, rows
):
    across = across_ref[...]
    pairs = [(tile, s) for tile in range(tiles) for s in range(4)]
    size = 64 * len(pairs)
    for g2 in range(2):
        for g0 in range(2):
            columns = []
            for tile, s in pairs:
                parts = [
                    x_ref[8 * g3 + 4 * g2 + 2 * g1 + g0, s, tile].reshape(16, 128) for g3 in range(2) for g1 in range(2)
                ]
                columns.append(jnp.concatenate(parts, axis=0))
            high, low = split(jnp.concatenate(columns, axis=1))
            moved = jnp.dot(across, jnp.concatenate([high, low, high], axis=0), preferred_element_type=jnp.float32)
            high, low = split(moved)
            lane = 128 * (2 * g2 + g0)
            for p in range(len(pairs)):
                rows[64 * p : 64 * p + 64, lane : lane + 128] = high[:, 128 * p : 128 * p + 128]
                rows[size + 64 * p : size + 64 * p + 64, lane : lane + 128] = low[:, 128 * p : 128 * p + 128]
    for t0 in range(2):
        wh, wl = high_ref[:, 256 * t0 : 256 * t0 + 256], low_ref[:, 256 * t0 : 256 * t0 + 256]
        both = jnp.dot(rows[...], wh, preferred_element_type=jnp.float32)
        total = both[:size] + both[size:] + jnp.dot(rows[:size], wl, preferred_element_type=jnp.float32)
        for p, (tile, s) in enumerate(pairs):
            cosine, sine = push_ref[tile, s, 0], push_ref[tile, s, 1]
            for t3 in range(2):
                for t1 in range(2):
                    at = 64 * p + 16 * t3 + 8 * t1
                    by_re, by_im = total[at : at + 8], total[at + 32 : at + 40]
                    real_re, real_im = by_re[:, :128], by_re[:, 128:]
                    imag_re, imag_im = by_im[:, :128], by_im[:, 128:]
                    for t2, real, imag in (
                        (0, real_re - imag_im, imag_re + real_im),
                        (1, real_re + imag_im, imag_re - real_im),
                    ):
                        low = t0 if t2 == 0 else 1 - t0
                        o_ref[4 * t3 + 2 * t2 + t1, tile, low, s, 0] = real * cosine - imag * sine
                        o_ref[4 * t3 + 2 * t2 + t1, tile, low, s, 1] = real * sine + imag * cosine


ANY = pl.BlockSpec(memory_space=pl.ANY)
LOOKUP = pltpu.SMEM((9, 64), jnp.float32)


def whole(shape):
    return pl.BlockSpec(shape, lambda i: (0,) * len(shape))


def pull(lookup, x):
    return pl.pallas_call(
        pull_kernel,
        out_shape=(
            jax.ShapeDtypeStruct((8, 8, 8, 2, 8, 128), jnp.float32),
            jax.ShapeDtypeStruct((8, 4, 2, 8, 128), jnp.float32),
        ),
        in_specs=[ANY, ANY],
        out_specs=(ANY, ANY),
        scratch_shapes=[
            LOOKUP,
            pltpu.SMEM((64,), jnp.int32),
            pltpu.VMEM((128, 2048), jnp.bfloat16),
            pltpu.VMEM((8, 64, 2, 8, 128), jnp.float32),
            pltpu.VMEM((8, 8, 8, 2, 8, 128), jnp.float32),
            pltpu.VMEM((8, 4, 2, 8, 128), jnp.float32),
            pltpu.VMEM((512, 2048), jnp.float32),
            pltpu.SemaphoreType.DMA,
            pltpu.SemaphoreType.DMA,
            pltpu.SemaphoreType.DMA((8,)),
            pltpu.SemaphoreType.DMA((8,)),
        ],
        compiler_params=pltpu.CompilerParams(vmem_limit_bytes=48 * 2**20),
    )(lookup, x)


def merge(push, x, tiles=4):
    high, low = down_matrix()
    return pl.pallas_call(
        lambda *refs: merge_kernel(tiles, *refs),
        grid=(8 // tiles,),
        out_shape=jax.ShapeDtypeStruct((8, 8, 2, 4, 2, 8, 128), jnp.float32),
        in_specs=[
            pl.BlockSpec((tiles, 4, 2, 8, 128), lambda i: (i, 0, 0, 0, 0)),
            whole((64, 192)),
            whole((512, 512)),
            whole((512, 512)),
            pl.BlockSpec((16, 4, tiles, 2, 8, 128), lambda i: (0, 0, i, 0, 0, 0)),
        ],
        out_specs=pl.BlockSpec((8, tiles, 2, 4, 2, 8, 128), lambda i: (0, i, 0, 0, 0, 0, 0)),
        scratch_shapes=[pltpu.VMEM((512 * tiles, 512), jnp.bfloat16)],
        compiler_params=pltpu.CompilerParams(vmem_limit_bytes=40 * 2**20),
    )(push, across_matrix(), high, low, x)


def local(weights_in, medium_speed, target_order):
    speeds = jnp.pad(medium_speed, ((0, 0), (0, 56)))
    lookup = jnp.concatenate([speeds, target_order.astype(jnp.float32)[None]], axis=0)
    turned, push = pull(lookup, weights_in[0])
    gathered = lax.all_to_all(turned.reshape(16, 4, 8, 2, 8, 128), WIDE, 0, 0, tiled=True)
    merged = merge(push, gathered)
    chunks = merged.reshape(128, 4, 2, 8, 128)
    spread = lax.all_to_all(chunks, ("z_hi", "y", "z_lo", "x", "core"), 0, 0, tiled=True)
    return spread.reshape(1, 8, 64, 2, 8, 128)


def solution(mesh):
    fine = Mesh(mesh.devices.reshape(FINE_SIZES), FINE)
    split_over = P(WIDE, NARROW, None, None, None, None)
    return jax.shard_map(local, mesh=fine, in_specs=(split_over, P(), P()), out_specs=split_over, check_vma=False)
```

```python
import numpy as np
import jax
import jax.numpy as jnp
from jax import lax
from jax.experimental import pallas as pl
from jax.experimental.pallas import tpu as pltpu
from jax.sharding import Mesh, PartitionSpec as P

SIN = (6.28318282, -41.3414214, 81.5961839, -76.5801007, 41.2053954, -12.2712631)
COS = (0.999999989, -19.7392045, 64.939119, -85.450166, 60.1678349, -25.9683235, 6.52962293)

NODES = 0.5 - 0.5 * np.cos(np.pi * (2.0 * np.arange(8) + 1.0) / 16.0)
TURNS = 16.0
FINE = ("z_hi", "y", "core", "z_lo", "x")
FINE_SIZES = (2, 4, 2, 2, 4)
WIDE, NARROW = FINE[:3], FINE[3:]


def lagrange(child):
    points = (child + NODES) / 2.0
    out = np.ones((8, 8))
    for q in range(8):
        for m in range(8):
            if m != q:
                out[q] *= (points - NODES[m]) / (NODES[q] - NODES[m])
    return out


def turn(amount):
    return np.exp(2j * np.pi * TURNS * amount)


def dimension_operator(boxes):
    out = np.zeros((2, 2, 8, 2, 2, 8), complex)
    for ta in range(2):
        for tb in range(2):
            da, db = (2 * ta - 1) / 32.0, (2 * tb - 1) / 64.0
            last = turn((da + db) * 4.0 * NODES / boxes)
            for ca in range(2):
                for cb in range(2):
                    first = lagrange(ca) * turn(-da * (2 * cb + ca + NODES) / boxes)
                    second = lagrange(cb) * turn(-db * (2 * cb + 2 * NODES) / boxes)
                    out[ta, tb, :, ca, cb, :] = last[:, None] * (second @ first)
    return out


def halves(matrix):
    matrix = matrix.astype(np.float32)
    high = matrix.astype(jnp.bfloat16)
    low = (matrix - high.astype(np.float32)).astype(jnp.bfloat16)
    return high, low


def across_matrix():
    op = dimension_operator(64)
    real = np.zeros((2, 2, 2, 8, 2, 2, 2, 8))
    real[0, ..., 0, :] = op.real
    real[0, ..., 1, :] = -op.imag
    real[1, ..., 0, :] = op.imag
    real[1, ..., 1, :] = op.real
    high, low = halves(real.reshape(64, 64))
    return np.concatenate([high, high, low], axis=1)


def down_matrix():
    move = np.transpose(dimension_operator(16), (3, 4, 5, 0, 1, 2))[:, :, :, 0]
    real = np.stack([move.real, move.imag], axis=4)
    return halves(np.kron(real.reshape(32, 32), np.eye(16)))


def horner(coefficients, x):
    total = jnp.full_like(x, coefficients[-1])
    for c in coefficients[-2::-1]:
        total = total * x + c
    return total


def unit(turns):
    rest = turns - jnp.round(turns)
    square = rest * rest
    return horner(COS, square), rest * horner(SIN, square)


def node_at(index):
    value = jnp.full(index.shape, NODES[0], jnp.float32)
    for q in range(1, 8):
        value = jnp.where(index == q, jnp.float32(NODES[q]), value)
    return value


def iota(axis):
    return lax.broadcasted_iota(jnp.int32, (8, 128), axis)


def tables(node_a, node_d, super_index, first, second, count):
    sa = (super_index // 4).astype(jnp.float32)
    sd = (super_index % 4).astype(jnp.float32)
    local_a = first + count * node_a - 2.0
    local_d = second + count * node_d - 2.0
    mid_a, mid_d = 4.0 * sa + 2.0, 4.0 * sd + 2.0
    off_a, off_d = local_a / 64.0, local_d / 16.0
    key_a, key_d = (mid_a + local_a) / 64.0, (mid_d + local_d) / 16.0
    base_a, base_d = mid_a / 64.0, mid_d / 16.0
    key = jnp.sqrt(key_a * key_a + key_d * key_d)
    base = jnp.sqrt(jnp.zeros_like(key) + (base_a * base_a + base_d * base_d))
    radial = (off_a * (key_a + base_a) + off_d * (key_d + base_d)) / (key + base)
    return TURNS * off_a, TURNS * off_d, TURNS * radial


def wide_code():
    return lax.axis_index("z_hi") * 8 + lax.axis_index("y") * 2 + lax.axis_index("core")


def narrow_place():
    return lax.axis_index("z_lo") * 4 + lax.axis_index("x")


def pull_kernel(
    order_hbm,
    speed_hbm,
    x_hbm,
    o_ref,
    push_ref,
    order_ref,
    speed_ref,
    place_ref,
    spread_ref,
    x_ref,
    turned,
    order_sem,
    speed_sem,
    in_sems,
):
    order_copy = pltpu.make_async_copy(order_hbm, order_ref, order_sem)
    speed_copy = pltpu.make_async_copy(speed_hbm, speed_ref, speed_sem)
    order_copy.start()
    speed_copy.start()
    arrivals = [pltpu.make_async_copy(x_hbm.at[s], x_ref.at[s], in_sems.at[s]) for s in range(8)]
    for arrival in arrivals:
        arrival.start()
    code = wide_code()
    bits = [(code >> k & 1).astype(jnp.float32) for k in range(4)]
    lane = iota(1)
    node_a, node_d = node_at(iota(0)), node_at(lane % 8)
    center_a = [(lane // 64 + 2 * high).astype(jnp.float32) / 8.0 + 0.0625 for high in range(4)]
    center_d = (lane // 8 % 8).astype(jnp.float32) / 8.0 + 0.0625
    plane, radial = [], []
    for s in range(8):
        super_index = narrow_place() * 8 + s
        table = tables(node_a, node_d, super_index, 2.0 * bits[1] + bits[3], 2.0 * bits[0] + bits[2], 1.0)
        plane.append([center_a[high] * table[0] + center_d * table[1] for high in range(4)])
        radial.append(table[2])
    spread_ref[...] = jnp.zeros_like(spread_ref)
    row = lax.broadcasted_iota(jnp.int32, (16, 128), 0)
    point = lax.broadcasted_iota(jnp.int32, (16, 128), 1) // 16
    for box in range(16):
        same = jnp.where(row == box % 2 * 8 + point, 1.0, 0.0).astype(jnp.bfloat16)
        spread_ref[box // 2 * 16 : box // 2 * 16 + 16, 128 * box : 128 * box + 128] = same
    order_copy.wait()
    speed_copy.wait()
    speed = []
    for high in range(4):
        value = jnp.zeros((8, 128), jnp.float32)
        for low in range(16):
            value = jnp.where(lane // 8 == low, speed_ref[2 * high + low // 8, low % 8], value)
        speed.append(value)
    for j in range(64):
        place_ref[order_ref[j]] = j % 8 * 64 + j // 8

    def spread(group):
        both_supers = (2 * group, 2 * group + 1)
        angles = [plane[s][high] + speed[high] * radial[s] for s in both_supers for high in range(4)]
        cosine, sine = unit(jnp.concatenate(angles, axis=0))
        high, low = split(jnp.concatenate([cosine[:32], sine[:32], cosine[32:], sine[32:]], axis=0))
        both = jnp.dot(jnp.concatenate([high, low], axis=0), spread_ref[...], preferred_element_type=jnp.float32)
        turned[128 * group : 128 * group + 128] = both[:128] + both[128:]

    spread(0)
    table = [
        tables(node_a, node_at(lane // 16), narrow_place() * 8 + code % 2 * 4 + s, 0.0, 0.0, 4.0) for s in range(4)
    ]
    for tile in range(8):
        box = order_ref[tile * 8 + code // 2]
        across = (box // 8).astype(jnp.float32) / 8.0 + 0.0625
        down = (box % 8).astype(jnp.float32) / 8.0 + 0.0625
        at_box = speed_ref[box // 8, box % 8]
        for s in range(4):
            cosine, sine = unit(across * table[s][0] + (down * table[s][1] + at_box * table[s][2]))
            push_ref[tile, s, 0] = cosine
            push_ref[tile, s, 1] = sine
    flat = o_ref.reshape(512, 2, 8, 128)
    for s in range(8):
        arrivals[s].wait()
        if s % 2 == 1 and s < 7:
            spread(s // 2 + 1)
        for box in range(64):
            place = place_ref[box] + 8 * s
            at, lanes = 64 * s + 8 * (box // 16), 128 * (box % 16)
            cosine = turned[at : at + 8, lanes : lanes + 128]
            sine = turned[32 + at : 40 + at, lanes : lanes + 128]
            real, imag = x_ref[s, box, 0], x_ref[s, box, 1]
            flat[place, 0] = real * cosine + imag * sine
            flat[place, 1] = imag * cosine - real * sine


def split(value):
    high = value.astype(jnp.bfloat16)
    return high, (value - high.astype(jnp.float32)).astype(jnp.bfloat16)


def merge_kernel(
    tiles, push_ref, across_ref, high_ref, low_ref, x_ref, o_ref, rows
):
    across = across_ref[...]
    for first in range(0, 8, tiles):
        merge_tiles(range(first, first + tiles), push_ref, across, high_ref, low_ref, x_ref, o_ref, rows)


def merge_tiles(steps, push_ref, across, high_ref, low_ref, x_ref, o_ref, rows):
    pairs = [(tile, s) for tile in steps for s in range(4)]
    size = 64 * len(pairs)
    for g2 in range(2):
        for g0 in range(2):
            columns = []
            for tile, s in pairs:
                parts = [
                    x_ref[8 * g3 + 4 * g2 + 2 * g1 + g0, s, tile].reshape(16, 128) for g3 in range(2) for g1 in range(2)
                ]
                columns.append(jnp.concatenate(parts, axis=0))
            high, low = split(jnp.concatenate(columns, axis=1))
            moved = jnp.dot(across, jnp.concatenate([high, low, high], axis=0), preferred_element_type=jnp.float32)
            high, low = split(moved)
            lane = 128 * (2 * g2 + g0)
            for p in range(len(pairs)):
                rows[64 * p : 64 * p + 64, lane : lane + 128] = high[:, 128 * p : 128 * p + 128]
                rows[size + 64 * p : size + 64 * p + 64, lane : lane + 128] = low[:, 128 * p : 128 * p + 128]
    for t0 in range(2):
        wh, wl = high_ref[:, 256 * t0 : 256 * t0 + 256], low_ref[:, 256 * t0 : 256 * t0 + 256]
        both = jnp.dot(rows[...], wh, preferred_element_type=jnp.float32)
        total = both[:size] + both[size:] + jnp.dot(rows[:size], wl, preferred_element_type=jnp.float32)
        for p, (tile, s) in enumerate(pairs):
            cosine, sine = push_ref[tile, s, 0], push_ref[tile, s, 1]
            for t3 in range(2):
                for t1 in range(2):
                    at = 64 * p + 16 * t3 + 8 * t1
                    by_re, by_im = total[at : at + 8], total[at + 32 : at + 40]
                    real_re, real_im = by_re[:, :128], by_re[:, 128:]
                    imag_re, imag_im = by_im[:, :128], by_im[:, 128:]
                    for t2, real, imag in (
                        (0, real_re - imag_im, imag_re + real_im),
                        (1, real_re + imag_im, imag_re - real_im),
                    ):
                        low = t0 if t2 == 0 else 1 - t0
                        o_ref[4 * t3 + 2 * t2 + t1, tile, low, s, 0] = real * cosine - imag * sine
                        o_ref[4 * t3 + 2 * t2 + t1, tile, low, s, 1] = real * sine + imag * cosine


ANY = pl.BlockSpec(memory_space=pl.ANY)
VMEM = pl.BlockSpec(memory_space=pltpu.VMEM)


def pull(order, speed, x):
    return pl.pallas_call(
        pull_kernel,
        out_shape=(
            jax.ShapeDtypeStruct((8, 8, 8, 2, 8, 128), jnp.float32),
            jax.ShapeDtypeStruct((8, 4, 2, 8, 128), jnp.float32),
        ),
        in_specs=[ANY, ANY, ANY],
        out_specs=(VMEM, VMEM),
        scratch_shapes=[
            pltpu.SMEM((64,), jnp.int32),
            pltpu.SMEM((8, 8), jnp.float32),
            pltpu.SMEM((64,), jnp.int32),
            pltpu.VMEM((128, 2048), jnp.bfloat16),
            pltpu.VMEM((8, 64, 2, 8, 128), jnp.float32),
            pltpu.VMEM((512, 2048), jnp.float32),
            pltpu.SemaphoreType.DMA,
            pltpu.SemaphoreType.DMA,
            pltpu.SemaphoreType.DMA((8,)),
        ],
        compiler_params=pltpu.CompilerParams(vmem_limit_bytes=48 * 2**20),
    )(order, speed, x)


def merge(push, x, tiles=2):
    high, low = down_matrix()
    return pl.pallas_call(
        lambda *refs: merge_kernel(tiles, *refs),
        out_shape=jax.ShapeDtypeStruct((8, 8, 2, 4, 2, 8, 128), jnp.float32),
        in_specs=[VMEM] * 5,
        out_specs=VMEM,
        scratch_shapes=[pltpu.VMEM((512 * tiles, 512), jnp.bfloat16)],
        compiler_params=pltpu.CompilerParams(vmem_limit_bytes=40 * 2**20),
    )(push, across_matrix(), high, low, x)


def local(weights_in, medium_speed, target_order):
    turned, push = pull(target_order, medium_speed, weights_in[0])
    gathered = lax.all_to_all(turned.reshape(16, 4, 8, 2, 8, 128), WIDE, 0, 0, tiled=True)
    merged = merge(push, gathered)
    chunks = merged.reshape(128, 4, 2, 8, 128)
    spread = lax.all_to_all(chunks, ("z_hi", "y", "z_lo", "x", "core"), 0, 0, tiled=True)
    return spread.reshape(1, 8, 64, 2, 8, 128)


def solution(mesh):
    fine = Mesh(mesh.devices.reshape(FINE_SIZES), FINE)
    split_over = P(WIDE, NARROW, None, None, None, None)
    return jax.shard_map(local, mesh=fine, in_specs=(split_over, P(), P()), out_specs=split_over, check_vma=False)
```

```python
import numpy as np
import jax
import jax.numpy as jnp
from jax import lax
from jax.experimental import pallas as pl
from jax.experimental.pallas import tpu as pltpu
from jax.sharding import Mesh, PartitionSpec as P

SIN = (6.28318282, -41.3414214, 81.5961839, -76.5801007, 41.2053954, -12.2712631)
COS = (0.999999989, -19.7392045, 64.939119, -85.450166, 60.1678349, -25.9683235, 6.52962293)

NODES = 0.5 - 0.5 * np.cos(np.pi * (2.0 * np.arange(8) + 1.0) / 16.0)
TURNS = 16.0
FINE = ("z_hi", "y", "core", "z_lo", "x")
FINE_SIZES = (2, 4, 2, 2, 4)
WIDE, NARROW = FINE[:3], FINE[3:]


def lagrange(child):
    points = (child + NODES) / 2.0
    out = np.ones((8, 8))
    for q in range(8):
        for m in range(8):
            if m != q:
                out[q] *= (points - NODES[m]) / (NODES[q] - NODES[m])
    return out


def turn(amount):
    return np.exp(2j * np.pi * TURNS * amount)


def dimension_operator(boxes):
    out = np.zeros((2, 2, 8, 2, 2, 8), complex)
    for ta in range(2):
        for tb in range(2):
            da, db = (2 * ta - 1) / 32.0, (2 * tb - 1) / 64.0
            last = turn((da + db) * 4.0 * NODES / boxes)
            for ca in range(2):
                for cb in range(2):
                    first = lagrange(ca) * turn(-da * (2 * cb + ca + NODES) / boxes)
                    second = lagrange(cb) * turn(-db * (2 * cb + 2 * NODES) / boxes)
                    out[ta, tb, :, ca, cb, :] = last[:, None] * (second @ first)
    return out


def halves(matrix):
    matrix = matrix.astype(np.float32)
    high = matrix.astype(jnp.bfloat16)
    low = (matrix - high.astype(np.float32)).astype(jnp.bfloat16)
    return high, low


def across_matrix():
    op = dimension_operator(64)
    real = np.zeros((2, 2, 2, 8, 2, 2, 2, 8))
    real[0, ..., 0, :] = op.real
    real[0, ..., 1, :] = -op.imag
    real[1, ..., 0, :] = op.imag
    real[1, ..., 1, :] = op.real
    high, low = halves(real.reshape(64, 64))
    return np.concatenate([high, high, low], axis=1)


def down_matrix():
    move = np.transpose(dimension_operator(16), (3, 4, 5, 0, 1, 2))[:, :, :, 0]
    real = np.stack([move.real, move.imag], axis=4)
    return halves(np.kron(real.reshape(32, 32), np.eye(16)))


def horner(coefficients, x):
    total = jnp.full_like(x, coefficients[-1])
    for c in coefficients[-2::-1]:
        total = total * x + c
    return total


def unit(turns):
    rest = turns - jnp.round(turns)
    square = rest * rest
    return horner(COS, square), rest * horner(SIN, square)


def node_at(index):
    value = jnp.full(index.shape, NODES[0], jnp.float32)
    for q in range(1, 8):
        value = jnp.where(index == q, jnp.float32(NODES[q]), value)
    return value


def iota(axis):
    return lax.broadcasted_iota(jnp.int32, (8, 128), axis)


def tables(node_a, node_d, super_index, first, second, count):
    sa = (super_index // 4).astype(jnp.float32)
    sd = (super_index % 4).astype(jnp.float32)
    local_a = first + count * node_a - 2.0
    local_d = second + count * node_d - 2.0
    mid_a, mid_d = 4.0 * sa + 2.0, 4.0 * sd + 2.0
    off_a, off_d = local_a / 64.0, local_d / 16.0
    key_a, key_d = (mid_a + local_a) / 64.0, (mid_d + local_d) / 16.0
    base_a, base_d = mid_a / 64.0, mid_d / 16.0
    key = jnp.sqrt(key_a * key_a + key_d * key_d)
    base = jnp.sqrt(jnp.zeros_like(key) + (base_a * base_a + base_d * base_d))
    radial = (off_a * (key_a + base_a) + off_d * (key_d + base_d)) / (key + base)
    return TURNS * off_a, TURNS * off_d, TURNS * radial


def wide_code():
    return lax.axis_index("z_hi") * 8 + lax.axis_index("y") * 2 + lax.axis_index("core")


def narrow_place():
    return lax.axis_index("z_lo") * 4 + lax.axis_index("x")


def pull_kernel(
    order_hbm,
    speed_hbm,
    x_hbm,
    o_ref,
    push_ref,
    order_ref,
    speed_ref,
    place_ref,
    spread_ref,
    x_ref,
    turned,
    order_sem,
    speed_sem,
    in_sems,
):
    order_copy = pltpu.make_async_copy(order_hbm, order_ref, order_sem)
    speed_copy = pltpu.make_async_copy(speed_hbm, speed_ref, speed_sem)
    order_copy.start()
    speed_copy.start()
    arrivals = [pltpu.make_async_copy(x_hbm.at[s], x_ref.at[s], in_sems.at[s]) for s in range(8)]
    for arrival in arrivals:
        arrival.start()
    code = wide_code()
    bits = [(code >> k & 1).astype(jnp.float32) for k in range(4)]
    lane = iota(1)
    node_a, node_d = node_at(iota(0)), node_at(lane % 8)
    center_a = [(lane // 64 + 2 * high).astype(jnp.float32) / 8.0 + 0.0625 for high in range(4)]
    center_d = (lane // 8 % 8).astype(jnp.float32) / 8.0 + 0.0625
    plane, radial = [], []
    for s in range(8):
        super_index = narrow_place() * 8 + s
        table = tables(node_a, node_d, super_index, 2.0 * bits[1] + bits[3], 2.0 * bits[0] + bits[2], 1.0)
        plane.append([center_a[high] * table[0] + center_d * table[1] for high in range(4)])
        radial.append(table[2])
    spread_ref[...] = jnp.zeros_like(spread_ref)
    row = lax.broadcasted_iota(jnp.int32, (16, 128), 0)
    point = lax.broadcasted_iota(jnp.int32, (16, 128), 1) // 16
    for box in range(16):
        same = jnp.where(row == box % 2 * 8 + point, 1.0, 0.0).astype(jnp.bfloat16)
        spread_ref[box // 2 * 16 : box // 2 * 16 + 16, 128 * box : 128 * box + 128] = same
    order_copy.wait()
    speed_copy.wait()
    speed = []
    for high in range(4):
        value = jnp.zeros((8, 128), jnp.float32)
        for low in range(16):
            value = jnp.where(lane // 8 == low, speed_ref[2 * high + low // 8, low % 8], value)
        speed.append(value)
    for j in range(64):
        place_ref[order_ref[j]] = j % 8 * 64 + j // 8

    def spread(group):
        both_supers = (2 * group, 2 * group + 1)
        angles = [plane[s][high] + speed[high] * radial[s] for s in both_supers for high in range(4)]
        cosine, sine = unit(jnp.concatenate(angles, axis=0))
        high, low = split(jnp.concatenate([cosine[:32], sine[:32], cosine[32:], sine[32:]], axis=0))
        both = jnp.dot(jnp.concatenate([high, low], axis=0), spread_ref[...], preferred_element_type=jnp.float32)
        turned[128 * group : 128 * group + 128] = both[:128] + both[128:]

    spread(0)
    table = [
        tables(node_a, node_at(lane // 16), narrow_place() * 8 + code % 2 * 4 + s, 0.0, 0.0, 4.0) for s in range(4)
    ]
    flat = o_ref.reshape(512, 2, 8, 128)
    for s in range(8):
        arrivals[s].wait()
        if s % 2 == 1 and s < 7:
            spread(s // 2 + 1)
        at_tile = order_ref[s * 8 + code // 2]
        across = (at_tile // 8).astype(jnp.float32) / 8.0 + 0.0625
        down = (at_tile % 8).astype(jnp.float32) / 8.0 + 0.0625
        at_box = speed_ref[at_tile // 8, at_tile % 8]
        turns = [across * part[0] + (down * part[1] + at_box * part[2]) for part in table]
        cosine, sine = unit(jnp.concatenate(turns, axis=0))
        for k in range(4):
            push_ref[s, k, 0] = cosine[8 * k : 8 * k + 8]
            push_ref[s, k, 1] = sine[8 * k : 8 * k + 8]
        for box in range(64):
            place = place_ref[box] + 8 * s
            at, lanes = 64 * s + 8 * (box // 16), 128 * (box % 16)
            cosine = turned[at : at + 8, lanes : lanes + 128]
            sine = turned[32 + at : 40 + at, lanes : lanes + 128]
            real, imag = x_ref[s, box, 0], x_ref[s, box, 1]
            flat[place, 0] = real * cosine + imag * sine
            flat[place, 1] = imag * cosine - real * sine


def split(value):
    high = value.astype(jnp.bfloat16)
    return high, (value - high.astype(jnp.float32)).astype(jnp.bfloat16)


def merge_kernel(
    tiles, push_ref, across_ref, high_ref, low_ref, x_ref, o_ref, rows
):
    across = across_ref[...]
    for first in range(0, 8, tiles):
        merge_tiles(range(first, first + tiles), push_ref, across, high_ref, low_ref, x_ref, o_ref, rows)


def merge_tiles(steps, push_ref, across, high_ref, low_ref, x_ref, o_ref, rows):
    pairs = [(tile, s) for tile in steps for s in range(4)]
    size = 64 * len(pairs)
    for g2 in range(2):
        for g0 in range(2):
            columns = []
            for tile, s in pairs:
                parts = [
                    x_ref[8 * g3 + 4 * g2 + 2 * g1 + g0, s, tile].reshape(16, 128) for g3 in range(2) for g1 in range(2)
                ]
                columns.append(jnp.concatenate(parts, axis=0))
            high, low = split(jnp.concatenate(columns, axis=1))
            moved = jnp.dot(across, jnp.concatenate([high, low, high], axis=0), preferred_element_type=jnp.float32)
            high, low = split(moved)
            lane = 128 * (2 * g2 + g0)
            for p in range(len(pairs)):
                rows[64 * p : 64 * p + 64, lane : lane + 128] = high[:, 128 * p : 128 * p + 128]
                rows[size + 64 * p : size + 64 * p + 64, lane : lane + 128] = low[:, 128 * p : 128 * p + 128]
    for t0 in range(2):
        wh, wl = high_ref[:, 256 * t0 : 256 * t0 + 256], low_ref[:, 256 * t0 : 256 * t0 + 256]
        both = jnp.dot(rows[...], wh, preferred_element_type=jnp.float32)
        total = both[:size] + both[size:] + jnp.dot(rows[:size], wl, preferred_element_type=jnp.float32)
        for p, (tile, s) in enumerate(pairs):
            cosine, sine = push_ref[tile, s, 0], push_ref[tile, s, 1]
            for t3 in range(2):
                for t1 in range(2):
                    at = 64 * p + 16 * t3 + 8 * t1
                    by_re, by_im = total[at : at + 8], total[at + 32 : at + 40]
                    real_re, real_im = by_re[:, :128], by_re[:, 128:]
                    imag_re, imag_im = by_im[:, :128], by_im[:, 128:]
                    for t2, real, imag in (
                        (0, real_re - imag_im, imag_re + real_im),
                        (1, real_re + imag_im, imag_re - real_im),
                    ):
                        low = t0 if t2 == 0 else 1 - t0
                        o_ref[4 * t3 + 2 * t2 + t1, tile, low, s, 0] = real * cosine - imag * sine
                        o_ref[4 * t3 + 2 * t2 + t1, tile, low, s, 1] = real * sine + imag * cosine


ANY = pl.BlockSpec(memory_space=pl.ANY)
VMEM = pl.BlockSpec(memory_space=pltpu.VMEM)


def pull(order, speed, x):
    return pl.pallas_call(
        pull_kernel,
        out_shape=(
            jax.ShapeDtypeStruct((8, 8, 8, 2, 8, 128), jnp.float32),
            jax.ShapeDtypeStruct((8, 4, 2, 8, 128), jnp.float32),
        ),
        in_specs=[ANY, ANY, ANY],
        out_specs=(VMEM, VMEM),
        scratch_shapes=[
            pltpu.SMEM((64,), jnp.int32),
            pltpu.SMEM((8, 8), jnp.float32),
            pltpu.SMEM((64,), jnp.int32),
            pltpu.VMEM((128, 2048), jnp.bfloat16),
            pltpu.VMEM((8, 64, 2, 8, 128), jnp.float32),
            pltpu.VMEM((512, 2048), jnp.float32),
            pltpu.SemaphoreType.DMA,
            pltpu.SemaphoreType.DMA,
            pltpu.SemaphoreType.DMA((8,)),
        ],
        compiler_params=pltpu.CompilerParams(vmem_limit_bytes=48 * 2**20),
    )(order, speed, x)


def merge(push, x, tiles=2):
    high, low = down_matrix()
    return pl.pallas_call(
        lambda *refs: merge_kernel(tiles, *refs),
        out_shape=jax.ShapeDtypeStruct((8, 8, 2, 4, 2, 8, 128), jnp.float32),
        in_specs=[VMEM] * 5,
        out_specs=VMEM,
        scratch_shapes=[pltpu.VMEM((512 * tiles, 512), jnp.bfloat16)],
        compiler_params=pltpu.CompilerParams(vmem_limit_bytes=40 * 2**20),
    )(push, across_matrix(), high, low, x)


def local(weights_in, medium_speed, target_order):
    turned, push = pull(target_order, medium_speed, weights_in[0])
    gathered = lax.all_to_all(turned.reshape(16, 4, 8, 2, 8, 128), WIDE, 0, 0, tiled=True)
    merged = merge(push, gathered)
    chunks = merged.reshape(128, 4, 2, 8, 128)
    spread = lax.all_to_all(chunks, ("z_hi", "y", "z_lo", "x", "core"), 0, 0, tiled=True)
    return spread.reshape(1, 8, 64, 2, 8, 128)


def solution(mesh):
    fine = Mesh(mesh.devices.reshape(FINE_SIZES), FINE)
    split_over = P(WIDE, NARROW, None, None, None, None)
    return jax.shard_map(local, mesh=fine, in_specs=(split_over, P(), P()), out_specs=split_over, check_vma=False)
```

```python
import numpy as np
import jax
import jax.numpy as jnp
from jax import lax
from jax.experimental import pallas as pl
from jax.experimental.pallas import tpu as pltpu
from jax.sharding import Mesh, PartitionSpec as P

SIN = (6.28318282, -41.3414214, 81.5961839, -76.5801007, 41.2053954, -12.2712631)
COS = (0.999999989, -19.7392045, 64.939119, -85.450166, 60.1678349, -25.9683235, 6.52962293)

NODES = 0.5 - 0.5 * np.cos(np.pi * (2.0 * np.arange(8) + 1.0) / 16.0)
TURNS = 16.0
FINE = ("z_hi", "y", "core", "z_lo", "x")
FINE_SIZES = (2, 4, 2, 2, 4)
WIDE, NARROW = FINE[:3], FINE[3:]


def lagrange(child):
    points = (child + NODES) / 2.0
    out = np.ones((8, 8))
    for q in range(8):
        for m in range(8):
            if m != q:
                out[q] *= (points - NODES[m]) / (NODES[q] - NODES[m])
    return out


def turn(amount):
    return np.exp(2j * np.pi * TURNS * amount)


def dimension_operator(boxes):
    out = np.zeros((2, 2, 8, 2, 2, 8), complex)
    for ta in range(2):
        for tb in range(2):
            da, db = (2 * ta - 1) / 32.0, (2 * tb - 1) / 64.0
            last = turn((da + db) * 4.0 * NODES / boxes)
            for ca in range(2):
                for cb in range(2):
                    first = lagrange(ca) * turn(-da * (2 * cb + ca + NODES) / boxes)
                    second = lagrange(cb) * turn(-db * (2 * cb + 2 * NODES) / boxes)
                    out[ta, tb, :, ca, cb, :] = last[:, None] * (second @ first)
    return out


def halves(matrix):
    matrix = matrix.astype(np.float32)
    high = matrix.astype(jnp.bfloat16)
    low = (matrix - high.astype(np.float32)).astype(jnp.bfloat16)
    return high, low


def across_matrix():
    op = dimension_operator(64)
    real = np.zeros((2, 2, 2, 8, 2, 2, 2, 8))
    real[0, ..., 0, :] = op.real
    real[0, ..., 1, :] = -op.imag
    real[1, ..., 0, :] = op.imag
    real[1, ..., 1, :] = op.real
    high, low = halves(real.reshape(64, 64))
    return np.concatenate([high, high, low], axis=1)


def down_matrix():
    move = np.transpose(dimension_operator(16), (3, 4, 5, 0, 1, 2))[:, :, :, 0]
    real = np.stack([move.real, move.imag], axis=4)
    return halves(np.kron(real.reshape(32, 32), np.eye(16)))


def horner(coefficients, x):
    total = jnp.full_like(x, coefficients[-1])
    for c in coefficients[-2::-1]:
        total = total * x + c
    return total


def unit(turns):
    rest = turns - jnp.round(turns)
    square = rest * rest
    return horner(COS, square), rest * horner(SIN, square)


def node_at(index):
    value = jnp.full(index.shape, NODES[0], jnp.float32)
    for q in range(1, 8):
        value = jnp.where(index == q, jnp.float32(NODES[q]), value)
    return value


def iota(axis):
    return lax.broadcasted_iota(jnp.int32, (8, 128), axis)


def tables(node_a, node_d, super_index, first, second, count):
    sa = (super_index // 4).astype(jnp.float32)
    sd = (super_index % 4).astype(jnp.float32)
    local_a = first + count * node_a - 2.0
    local_d = second + count * node_d - 2.0
    mid_a, mid_d = 4.0 * sa + 2.0, 4.0 * sd + 2.0
    off_a, off_d = local_a / 64.0, local_d / 16.0
    key_a, key_d = (mid_a + local_a) / 64.0, (mid_d + local_d) / 16.0
    base_a, base_d = mid_a / 64.0, mid_d / 16.0
    key = jnp.sqrt(key_a * key_a + key_d * key_d)
    base = jnp.sqrt(jnp.zeros_like(key) + (base_a * base_a + base_d * base_d))
    radial = (off_a * (key_a + base_a) + off_d * (key_d + base_d)) / (key + base)
    return TURNS * off_a, TURNS * off_d, TURNS * radial


def wide_code():
    return lax.axis_index("z_hi") * 8 + lax.axis_index("y") * 2 + lax.axis_index("core")


def narrow_place():
    return lax.axis_index("z_lo") * 4 + lax.axis_index("x")


def pull_kernel(
    order_hbm,
    speed_hbm,
    x_hbm,
    o_ref,
    push_ref,
    order_ref,
    speed_ref,
    place_ref,
    spread_ref,
    x_ref,
    turned,
    order_sem,
    speed_sem,
    in_sems,
):
    order_copy = pltpu.make_async_copy(order_hbm, order_ref, order_sem)
    speed_copy = pltpu.make_async_copy(speed_hbm, speed_ref, speed_sem)
    order_copy.start()
    speed_copy.start()
    arrivals = [pltpu.make_async_copy(x_hbm.at[s], x_ref.at[s], in_sems.at[s]) for s in range(8)]
    for arrival in arrivals:
        arrival.start()
    code = wide_code()
    bits = [(code >> k & 1).astype(jnp.float32) for k in range(4)]
    lane = iota(1)
    node_a, node_d = node_at(iota(0)), node_at(lane % 8)
    center_a = [(lane // 64 + 2 * high).astype(jnp.float32) / 8.0 + 0.0625 for high in range(4)]
    center_d = (lane // 8 % 8).astype(jnp.float32) / 8.0 + 0.0625
    plane, radial = [], []
    for s in range(8):
        super_index = narrow_place() * 8 + s
        table = tables(node_a, node_d, super_index, 2.0 * bits[1] + bits[3], 2.0 * bits[0] + bits[2], 1.0)
        plane.append([center_a[high] * table[0] + center_d * table[1] for high in range(4)])
        radial.append(table[2])
    spread_ref[...] = jnp.zeros_like(spread_ref)
    row = lax.broadcasted_iota(jnp.int32, (16, 128), 0)
    point = lax.broadcasted_iota(jnp.int32, (16, 128), 1) // 16
    for box in range(16):
        same = jnp.where(row == box % 2 * 8 + point, 1.0, 0.0).astype(jnp.bfloat16)
        spread_ref[box // 2 * 16 : box // 2 * 16 + 16, 128 * box : 128 * box + 128] = same
    order_copy.wait()
    speed_copy.wait()
    speed = []
    for high in range(4):
        value = jnp.zeros((8, 128), jnp.float32)
        for low in range(16):
            value = jnp.where(lane // 8 == low, speed_ref[2 * high + low // 8, low % 8], value)
        speed.append(value)
    for j in range(64):
        place_ref[order_ref[j]] = j % 8 * 64 + j // 8

    def spread(group):
        both_supers = (2 * group, 2 * group + 1)
        angles = [plane[s][high] + speed[high] * radial[s] for s in both_supers for high in range(4)]
        cosine, sine = unit(jnp.concatenate(angles, axis=0))
        high, low = split(jnp.concatenate([cosine[:32], sine[:32], cosine[32:], sine[32:]], axis=0))
        both = jnp.dot(jnp.concatenate([high, low], axis=0), spread_ref[...], preferred_element_type=jnp.float32)
        turned[128 * group : 128 * group + 128] = both[:128] + both[128:]

    spread(0)
    table = [
        tables(node_a, node_at(lane // 16), narrow_place() * 8 + code % 2 * 4 + s, 0.0, 0.0, 4.0) for s in range(4)
    ]
    for tile in range(8):
        box = order_ref[tile * 8 + code // 2]
        across = (box // 8).astype(jnp.float32) / 8.0 + 0.0625
        down = (box % 8).astype(jnp.float32) / 8.0 + 0.0625
        at_box = speed_ref[box // 8, box % 8]
        for s in range(4):
            cosine, sine = unit(across * table[s][0] + (down * table[s][1] + at_box * table[s][2]))
            push_ref[tile, s, 0] = cosine
            push_ref[tile, s, 1] = sine
    flat = o_ref.reshape(512, 2, 8, 128)
    for group in range(4):
        for s in (2 * group, 2 * group + 1):
            arrivals[s].wait()
        if group < 3:
            spread(group + 1)
        for box in range(64):
            place = place_ref[box]
            for s in (2 * group, 2 * group + 1):
                at, lanes = 64 * s + 8 * (box // 16), 128 * (box % 16)
                cosine = turned[at : at + 8, lanes : lanes + 128]
                sine = turned[32 + at : 40 + at, lanes : lanes + 128]
                real, imag = x_ref[s, box, 0], x_ref[s, box, 1]
                flat[place + 8 * s, 0] = real * cosine + imag * sine
                flat[place + 8 * s, 1] = imag * cosine - real * sine


def split(value):
    high = value.astype(jnp.bfloat16)
    return high, (value - high.astype(jnp.float32)).astype(jnp.bfloat16)


def merge_kernel(
    tiles, push_ref, across_ref, high_ref, low_ref, x_ref, o_ref, rows
):
    across = across_ref[...]
    for first in range(0, 8, tiles):
        merge_tiles(range(first, first + tiles), push_ref, across, high_ref, low_ref, x_ref, o_ref, rows)


def merge_tiles(steps, push_ref, across, high_ref, low_ref, x_ref, o_ref, rows):
    pairs = [(tile, s) for tile in steps for s in range(4)]
    size = 64 * len(pairs)
    for g2 in range(2):
        for g0 in range(2):
            columns = []
            for tile, s in pairs:
                parts = [
                    x_ref[8 * g3 + 4 * g2 + 2 * g1 + g0, s, tile].reshape(16, 128) for g3 in range(2) for g1 in range(2)
                ]
                columns.append(jnp.concatenate(parts, axis=0))
            high, low = split(jnp.concatenate(columns, axis=1))
            moved = jnp.dot(across, jnp.concatenate([high, low, high], axis=0), preferred_element_type=jnp.float32)
            high, low = split(moved)
            lane = 128 * (2 * g2 + g0)
            for p in range(len(pairs)):
                rows[64 * p : 64 * p + 64, lane : lane + 128] = high[:, 128 * p : 128 * p + 128]
                rows[size + 64 * p : size + 64 * p + 64, lane : lane + 128] = low[:, 128 * p : 128 * p + 128]
    for t0 in range(2):
        wh, wl = high_ref[:, 256 * t0 : 256 * t0 + 256], low_ref[:, 256 * t0 : 256 * t0 + 256]
        both = jnp.dot(rows[...], wh, preferred_element_type=jnp.float32)
        total = both[:size] + both[size:] + jnp.dot(rows[:size], wl, preferred_element_type=jnp.float32)
        for p, (tile, s) in enumerate(pairs):
            cosine, sine = push_ref[tile, s, 0], push_ref[tile, s, 1]
            for t3 in range(2):
                for t1 in range(2):
                    at = 64 * p + 16 * t3 + 8 * t1
                    by_re, by_im = total[at : at + 8], total[at + 32 : at + 40]
                    real_re, real_im = by_re[:, :128], by_re[:, 128:]
                    imag_re, imag_im = by_im[:, :128], by_im[:, 128:]
                    for t2, real, imag in (
                        (0, real_re - imag_im, imag_re + real_im),
                        (1, real_re + imag_im, imag_re - real_im),
                    ):
                        low = t0 if t2 == 0 else 1 - t0
                        o_ref[4 * t3 + 2 * t2 + t1, tile, low, s, 0] = real * cosine - imag * sine
                        o_ref[4 * t3 + 2 * t2 + t1, tile, low, s, 1] = real * sine + imag * cosine


ANY = pl.BlockSpec(memory_space=pl.ANY)
VMEM = pl.BlockSpec(memory_space=pltpu.VMEM)


def pull(order, speed, x):
    return pl.pallas_call(
        pull_kernel,
        out_shape=(
            jax.ShapeDtypeStruct((8, 8, 8, 2, 8, 128), jnp.float32),
            jax.ShapeDtypeStruct((8, 4, 2, 8, 128), jnp.float32),
        ),
        in_specs=[ANY, ANY, ANY],
        out_specs=(VMEM, VMEM),
        scratch_shapes=[
            pltpu.SMEM((64,), jnp.int32),
            pltpu.SMEM((8, 8), jnp.float32),
            pltpu.SMEM((64,), jnp.int32),
            pltpu.VMEM((128, 2048), jnp.bfloat16),
            pltpu.VMEM((8, 64, 2, 8, 128), jnp.float32),
            pltpu.VMEM((512, 2048), jnp.float32),
            pltpu.SemaphoreType.DMA,
            pltpu.SemaphoreType.DMA,
            pltpu.SemaphoreType.DMA((8,)),
        ],
        compiler_params=pltpu.CompilerParams(vmem_limit_bytes=48 * 2**20),
    )(order, speed, x)


def merge(push, x, tiles=2):
    high, low = down_matrix()
    return pl.pallas_call(
        lambda *refs: merge_kernel(tiles, *refs),
        out_shape=jax.ShapeDtypeStruct((8, 8, 2, 4, 2, 8, 128), jnp.float32),
        in_specs=[VMEM] * 5,
        out_specs=VMEM,
        scratch_shapes=[pltpu.VMEM((512 * tiles, 512), jnp.bfloat16)],
        compiler_params=pltpu.CompilerParams(vmem_limit_bytes=40 * 2**20),
    )(push, across_matrix(), high, low, x)


def local(weights_in, medium_speed, target_order):
    turned, push = pull(target_order, medium_speed, weights_in[0])
    gathered = lax.all_to_all(turned.reshape(16, 4, 8, 2, 8, 128), WIDE, 0, 0, tiled=True)
    merged = merge(push, gathered)
    chunks = merged.reshape(128, 4, 2, 8, 128)
    spread = lax.all_to_all(chunks, ("z_hi", "y", "z_lo", "x", "core"), 0, 0, tiled=True)
    return spread.reshape(1, 8, 64, 2, 8, 128)


def solution(mesh):
    fine = Mesh(mesh.devices.reshape(FINE_SIZES), FINE)
    split_over = P(WIDE, NARROW, None, None, None, None)
    return jax.shard_map(local, mesh=fine, in_specs=(split_over, P(), P()), out_specs=split_over, check_vma=False)
```
